512 devices in a mesh: sky: 128 (over z, x, core), tm: 4 (over y).
Axes of the slice: x: 4, y: 4, z: 16, core: 2. Of those that a mesh axis runs over, the one named last changes fastest.
Arguments:
- star_pos: float32 [1024, 3, 512], P(('sky', 'tm'))
- noise_var: float32 [1024, 512], P(('sky', 'tm')), may hold values from 0.5 to 2
- targets: float32 [1024, 64, 512], P(('sky', 'tm'))
- pair_list: int32 [1024, 14], P(('sky', 'tm')), may hold values from -1 to 1023, as said below
Outputs:
- solution: float32 [1024, 64, 512], P(('sky', 'tm'))
- residual: float32 [1024, 64, 512], P(('sky', 'tm'))
The draws below stay inside these ranges and needn't reach their ends.
Inputs may be any that keep to these rules, and one draw needn't show every extreme that they name: `pair_list`: row g lists first the ids of the blocks whose pair with g is evaluated at g, then -1 in the remaining slots. Each evaluated pair of distinct blocks is listed exactly once, at one of its two blocks, and only the listed pairs take part in the operator; a listed partner lies on the same device or on a device adjacent along sky, along tm or both.
All inputs are finite; a program needn't handle non-finite values.
Results may differ from the reference program's by a relative error of at most 0.00035.
Values sent between devices are 32-bit elements; how exact they have to be, the bound alone decides.
No kernel may reach another device: no remote copies, remote signals or barrier semaphores. Data moves between devices by JAX's collectives and lax.ppermute only.
A program may use at most 64 MiB of HBM per device.

```python
import math
import jax
import jax.numpy as jnp
from jax import lax

BPD = 2
BLK = 512
W = 64
PAIRS = 14
ITERS = 2
NBLK = 1024
N_SKY = 128
N_TM = 4


def draw_star_pos(key, part):
    key = jax.random.fold_in(key, 3)
    keys = jax.random.split(key, 3)
    block_ids = jnp.arange(NBLK, dtype=jnp.int32)
    device = block_ids // BPD
    column = device // N_TM * BPD + block_ids % BPD
    epoch = device % N_TM
    spread = (BLK / 5.0) ** 0.5
    first = jax.random.uniform(keys[0], (NBLK, BLK), jnp.float32, 0.0, 0.999)
    second = jax.random.uniform(keys[1], (NBLK, BLK), jnp.float32, 0.0, 0.999)
    third = jax.random.uniform(keys[2], (NBLK, BLK), jnp.float32, 0.0, 0.999)
    along = (column[:, None].astype(jnp.float32) + first) * 0.5
    across = second * spread
    times = (epoch[:, None].astype(jnp.float32) + third) * spread
    return jnp.stack([along, across, times], axis=1)


def draw_targets(key, part):
    key = jax.random.fold_in(key, 5)
    keys = jax.random.split(key, 3)
    block_ids = jnp.arange(NBLK, dtype=jnp.float32)
    growth = 1.0 + 2.0 * block_ids / max(NBLK - 1, 1)
    values = jax.random.normal(keys[2], (NBLK, W, BLK), jnp.float32)
    values = jnp.clip(values, -6.0, 6.0)
    return values * growth[:, None, None]


def neighbour(column, epoch, shift_col, shift_epoch):
    cells = N_SKY * BPD
    new_col = column + shift_col
    new_epoch = epoch + shift_epoch
    valid = (new_col >= 0) & (new_col < cells) & (new_epoch >= 0) & (new_epoch < N_TM)
    safe_col = jnp.clip(new_col, 0, cells - 1)
    safe_epoch = jnp.clip(new_epoch, 0, N_TM - 1)
    ident = (safe_col // BPD * N_TM + safe_epoch) * BPD + safe_col % BPD
    return (valid, ident.astype(jnp.int32))


def draw_pair_list(key, part):
    key = jax.random.fold_in(key, 11)
    block_ids = jnp.arange(NBLK, dtype=jnp.int32)
    device = block_ids // BPD
    column = device // N_TM * BPD + block_ids % BPD
    epoch = device % N_TM
    last = NBLK - 1
    forward = [(-2, 1), (-1, 1), (0, 1), (1, 1), (2, 1), (1, 0), (2, 0)]
    coins = jax.random.randint(key, (NBLK, len(forward)), 0, 3)
    columns_out = []
    for number, (shift_col, shift_epoch) in enumerate(forward):
        valid, partner = neighbour(column, epoch, shift_col, shift_epoch)
        at_self = valid & ((coins[:, number] == 1) | (partner == last)) & (block_ids != last)
        columns_out.append(jnp.where(at_self, partner, -1))
    for number, (shift_col, shift_epoch) in enumerate(forward):
        valid, source = neighbour(column, epoch, -shift_col, -shift_epoch)
        source_keeps = ((coins[source, number] == 1) | (block_ids == last)) & (source != last)
        dropped = (coins[source, number] == 2) & (block_ids != last) & (source != last)
        at_self = valid & jnp.logical_not(source_keeps) & jnp.logical_not(dropped)
        columns_out.append(jnp.where(at_self, source, -1))
    entries = jnp.stack(columns_out, axis=1).astype(jnp.int32)
    order = jnp.argsort(jnp.where(entries >= 0, 0, 1), axis=1, stable=True)
    return jnp.take_along_axis(entries, order, axis=1)


def steps_of(own_key, dims, cuts, least, largest):
    def one(dim, blocks):
        draws = jax.random.uniform(jax.random.fold_in(jax.random.fold_in(own_key, 6), dim), (blocks,), jnp.float32, least / len(cuts), largest / len(cuts))
        return jnp.repeat(jnp.exp(draws), dims[dim] // blocks).reshape((-1,) + (1,) * (len(dims) - dim - 1))

    gain = one(*cuts[0])
    for cut in cuts[1:]:
        gain = gain * one(*cut)
    return gain


def setup_inputs(seed: int = 0) -> dict:
    streams_of = jax.random.split(jax.random.key(seed), 5)
    return {
        "star_pos": draw_star_pos(jax.random.fold_in(streams_of[4], 71), 0),
        "noise_var": jnp.clip(jnp.exp(math.log(2.0) - 1.3862944 * jax.random.uniform(streams_of[1], (NBLK, BLK), jnp.float32) ** steps_of(streams_of[1], (NBLK, BLK), ((0, 512),), -0.2, 0.2)), 0.5, 2.0),
        "targets": draw_targets(jax.random.fold_in(streams_of[4], 71), 0),
        "pair_list": draw_pair_list(jax.random.fold_in(streams_of[4], 71), 0),
    }


def kernel_tile(left_pos, right_pos):
    squared = jnp.zeros((left_pos.shape[1], right_pos.shape[1]), jnp.float32)
    for component in range(3):
        offset = left_pos[component][:, None] - right_pos[component][None, :]
        squared = squared + offset * offset
    radius = jnp.sqrt(squared)
    margin = jnp.maximum(1.0 - radius, 0.0)
    margin_sq = margin * margin
    return margin_sq * margin_sq * (4.0 * radius + 1.0) * 0.3

def pull(vector, panel):
    return lax.dot_general(vector, panel, (((1,), (1,)), ((), ())), precision=lax.Precision.HIGHEST)

def push(vector, panel):
    return lax.dot_general(vector, panel, (((1,), (0,)), ((), ())), precision=lax.Precision.HIGHEST)

def operator(star_pos, noise_var, pair_list, vector):

    def visit(result, block_at):
        own_pos = star_pos[block_at]
        own_vec = vector[block_at]
        result = result.at[block_at].add(pull(own_vec, kernel_tile(own_pos, own_pos)))

        def slot(slot_at, result):
            partner = pair_list[block_at, slot_at]
            live = (partner >= 0).astype(jnp.float32)
            target = jnp.maximum(partner, 0).astype(jnp.int32)
            panel = kernel_tile(own_pos, star_pos[target]) * live
            result = result.at[block_at].add(pull(vector[target], panel))
            return result.at[target].add(push(own_vec, panel))
        return (lax.fori_loop(0, PAIRS, slot, result), block_at)
    start = noise_var[:, None, :] * vector
    result, visited = lax.scan(visit, start, jnp.arange(NBLK, dtype=jnp.int32))
    return result

def reference(star_pos, noise_var, targets, pair_list):
    solution = jnp.zeros_like(targets)
    residual = targets
    direction = targets
    norm_now = lax.optimization_barrier(jnp.sum(residual * residual, axis=(0, 2)))
    for iteration in range(ITERS):
        image = operator(star_pos, noise_var, pair_list, direction)
        alpha = norm_now / lax.optimization_barrier(jnp.sum(direction * image, axis=(0, 2)))
        solution = solution + alpha[None, :, None] * direction
        residual = residual - alpha[None, :, None] * image
        norm_next = lax.optimization_barrier(jnp.sum(residual * residual, axis=(0, 2)))
        direction = residual + (norm_next / norm_now)[None, :, None] * direction
        norm_now = norm_next
    return (solution, residual)
```

```python
import functools

import jax
import jax.numpy as jnp
from jax import lax
from jax.experimental import pallas as pl
from jax.experimental.pallas import tpu as pltpu
from jax.sharding import Mesh, PartitionSpec as P

F32 = jnp.float32
BF16 = jnp.bfloat16
BLOCKS, WIDTH, STARS, LANES = 2, 64, 512, 128
CHUNKS = STARS // LANES
POS, NOISE, LIST, IDENT, ROWS = 64, 67, 68, 69, 72
NEAR = 18
OWN = 8
TABLE_ROWS = 24
LONG, SHORT = 256, 64
PADDED = STARS + LONG
VMEM = pl.BlockSpec(memory_space=pltpu.VMEM)
SMEM = pl.BlockSpec(memory_space=pltpu.SMEM)
LIMIT = 48 * 1024 * 1024


def nt(left, right):
    return lax.dot_general(left, right, (((1,), (1,)), ((), ())), preferred_element_type=F32)


def nn(left, right):
    return lax.dot_general(left, right, (((1,), (0,)), ((), ())), preferred_element_type=F32)


def iota(shape, dim):
    return lax.broadcasted_iota(jnp.int32, shape, dim)


def column(row):
    return jnp.transpose(jnp.broadcast_to(row, (LANES, LANES)))


def lanes(chunk):
    return slice(chunk * LANES, (chunk + 1) * LANES)


def split_three(x):
    top = x.astype(BF16)
    rest = x - top.astype(F32)
    middle = rest.astype(BF16)
    return top, middle, (rest - middle.astype(F32)).astype(BF16)


def split_two(x):
    top = x.astype(BF16)
    return top, (x - top.astype(F32)).astype(BF16)


def one_hot(rank):
    same = iota((STARS, STARS), 0) == rank.astype(jnp.int32)
    return jnp.where(same, 1.0, 0.0).astype(BF16)


def unsort(x, rank):
    parts = nn(jnp.concatenate(split_three(x), axis=0), one_hot(rank))
    return (parts[:WIDTH] + parts[WIDTH : 2 * WIDTH]) + parts[2 * WIDTH :]


def sort_kernel(ident_ref, pos_ref, noise_ref, targets_ref, list_ref, packed_ref, rank_ref, stage):
    height = stage.shape[0]
    for b in range(BLOCKS):
        times = pos_ref[b, 2:3, :]
        counts = [jnp.zeros((1, LANES), F32) for _ in range(CHUNKS)]
        for jc in range(CHUNKS):
            other = column(times[:, lanes(jc)])
            for ic in range(CHUNKS):
                mine = times[:, lanes(ic)]
                if jc < ic:
                    before = other <= mine
                elif jc > ic:
                    before = other < mine
                else:
                    earlier = iota((LANES, LANES), 0) < iota((LANES, LANES), 1)
                    before = (other < mine) | ((other == mine) & earlier)
                counts[ic] += jnp.sum(jnp.where(before, 1.0, 0.0), axis=0, keepdims=True)
        rank = jnp.concatenate(counts, axis=1)
        rank_ref[b : b + 1, :] = rank
        stage[0:WIDTH, :] = targets_ref[b]
        stage[WIDTH:, :] = jnp.zeros((height - WIDTH, STARS), F32)
        stage[POS : POS + 3, :] = pos_ref[b]
        stage[NOISE : NOISE + 1, :] = noise_ref[b : b + 1, :]
        parts = nt(jnp.concatenate(split_three(stage[...]), axis=0), one_hot(rank))
        placed = (parts[:height] + parts[height : 2 * height]) + parts[2 * height :]
        packed_ref[b] = placed[:ROWS]
        listed = list_ref[b : b + 1, :].astype(F32) + 1.0
        packed_ref[b, LIST : LIST + 1, 0 : listed.shape[1]] = listed
        packed_ref[b, IDENT : IDENT + 1, :] = jnp.full((1, STARS), (ident_ref[0] + b + 1).astype(F32))


def build_table(near, table, times, lists, idents):
    for scratch in (times, lists, idents):
        scratch[...] = jnp.zeros(scratch.shape, F32)
    for k in range(NEAR):
        block = near(k)
        times[k : k + 1, :] = block[POS + 2 : POS + 3, :]
        lists[k : k + 1, :] = block[LIST : LIST + 1, 0:LANES]
        idents[k : k + 1, :] = block[IDENT : IDENT + 1, 0:LANES]
    place = iota((TABLE_ROWS, LANES), 1)
    out = jnp.zeros((TABLE_ROWS, LANES), jnp.int32)
    ident = idents[:, 0:1]
    for o in range(BLOCKS):
        own_ident = idents[OWN + o : OWN + o + 1, 0:1]
        own_list = lists[OWN + o : OWN + o + 1, :]
        own_list = jnp.where(own_list == 0.0, -5.0, own_list)
        hit = jnp.where((lists[...] == own_ident) | (own_list == ident), 1.0, 0.0)
        linked = (jnp.max(hit, axis=1, keepdims=True) > 0.0) | (ident == own_ident)
        mine = times[OWN + o : OWN + o + 1, :]
        total = jnp.zeros((TABLE_ROWS, 1), jnp.int32)
        for jc in range(CHUNKS):
            first = times[:, jc * LANES : jc * LANES + 1]
            last = times[:, (jc + 1) * LANES - 1 : (jc + 1) * LANES]
            skipped = jnp.sum(jnp.where(first - mine >= 1.0, 1.0, 0.0), axis=1, keepdims=True)
            beyond = jnp.sum(jnp.where(mine - last >= 1.0, 1.0, 0.0), axis=1, keepdims=True)
            start = skipped.astype(jnp.int32)
            end = STARS - beyond.astype(jnp.int32)
            aligned = start - (start & 7)
            count = jnp.where(linked & (end > start), end - aligned, 0)
            total = total + count
            col = 2 * (o * CHUNKS + jc)
            out = jnp.where(place == col, aligned, out)
            out = jnp.where(place == col + 1, count, out)
        out = jnp.where(place == 4 * CHUNKS + o, total, out)
    table[...] = out


def stage_weights(values, weights):
    def one(k, _):
        top, rest = split_two(values(k))
        for jc in range(CHUNKS):
            at = k * CHUNKS + jc
            weights[at, 0:WIDTH, 0:LANES] = top[:, lanes(jc)]
            weights[at, 0:WIDTH, LANES:] = top[:, lanes(jc)]
            weights[at, WIDTH:, 0:LANES] = rest[:, lanes(jc)]
            weights[at, WIDTH:, LANES:] = jnp.zeros((WIDTH, LANES), BF16)
        return 0

    return one


def tile_step(o, at, start, rows, own_pos, places, weights, total):
    start = pl.multiple_of(start, 8)
    squared = None
    for c in range(3):
        offset = own_pos[o, c, pl.ds(start, rows), :] - places[at, c : c + 1, :]
        squared = offset * offset if squared is None else squared + offset * offset
    radius = squared * lax.rsqrt(jnp.maximum(squared, 1e-30))
    margin = jnp.maximum(1.0 - radius, 0.0)
    margin_sq = margin * margin
    tile = (margin_sq * margin_sq) * (1.2 * radius + 0.3)
    both = jnp.concatenate(split_two(tile), axis=1)
    total[o, pl.ds(start, rows), :] += nt(both, weights[at])


def run_pairs(table, own_pos, places, weights, total):
    for o in range(BLOCKS):
        for c in range(3):
            for ic in range(CHUNKS):
                row = places[(OWN + o) * CHUNKS + ic, c : c + 1, :]
                own_pos[o, c, lanes(ic), :] = column(row)
            own_pos[o, c, STARS:, :] = jnp.zeros((PADDED - STARS, LANES), F32)
    total[...] = jnp.zeros(total.shape, F32)

    def per_block(k, _):
        for o in range(BLOCKS):

            @pl.when(table[k, 4 * CHUNKS + o] > 0)
            def _():
                for jc in range(CHUNKS):
                    col = 2 * (o * CHUNKS + jc)
                    start, count = table[k, col], table[k, col + 1]
                    at = k * CHUNKS + jc
                    whole = (count + (LONG - SHORT - 1)) // LONG

                    def step(i, _):
                        tile_step(o, at, start + LONG * i, LONG, own_pos, places, weights, total)
                        return 0

                    lax.fori_loop(0, whole, step, 0)

                    @pl.when(count > LONG * whole)
                    def _():
                        tile_step(o, at, start + LONG * whole, SHORT, own_pos, places, weights, total)

        return 0

    lax.fori_loop(0, NEAR, per_block, 0)


def image_of(o, total, places, vector):
    folded = jnp.transpose(total[o, 0:STARS, :])
    noise = jnp.concatenate(
        [places[(OWN + o) * CHUNKS + ic, NOISE - POS : NOISE - POS + 1, :] for ic in range(CHUNKS)], axis=1
    )
    return noise * vector + (folded[:WIDTH] + folded[WIDTH:])


def first_kernel(
    low, mid, high, image_ref, places, table, weights, own_pos, total, times, lists, idents, scalars, sem
):
    groups = (low, mid, high)

    def near(k):
        return groups[k // 6].at[k % 6]

    build_table(near, table, times, lists, idents)
    copy = pltpu.make_async_copy(table, scalars, sem)
    copy.start()
    for g, group in enumerate(groups):

        def one(i, _):
            k = 6 * g + i
            for jc in range(CHUNKS):
                places[k * CHUNKS + jc] = group[i, POS:ROWS, lanes(jc)]
            return stage_weights(lambda at: group[i, 0:WIDTH, :], weights)(k, 0)

        lax.fori_loop(0, 6, one, 0)
    copy.wait()
    run_pairs(scalars, own_pos, places, weights, total)
    for o in range(BLOCKS):
        image_ref[o] = image_of(o, total, places, mid[2 + o, 0:WIDTH, :])


def second_kernel(
    table, low, mid, high, places, packed, rank, image_ref, moments_ref, weights, own_pos, total, square
):
    groups = (low, mid, high)
    for g, group in enumerate(groups):
        one = stage_weights(lambda k: group[k - 6 * g], weights)
        lax.fori_loop(6 * g, 6 * g + 6, one, 0)
    run_pairs(table, own_pos, places, weights, total)
    sums = [jnp.zeros((WIDTH, LANES), F32) for _ in range(5)]
    for o in range(BLOCKS):
        start, once = packed[o, 0:WIDTH, :], mid[2 + o]
        twice = image_of(o, total, places, once)
        image_ref[o] = unsort(twice, rank[o : o + 1, :])
        products = (start * start, start * once, once * once, start * twice, once * twice)
        for n, product in enumerate(products):
            for ic in range(CHUNKS):
                sums[n] += product[:, lanes(ic)]
    square[...] = jnp.zeros(square.shape, F32)
    for n in range(5):
        square[0:WIDTH, n : n + 1] = jnp.sum(sums[n], axis=1, keepdims=True)
    turned = jnp.transpose(square[...])[0:8, :]
    top, middle, rest = (part.astype(F32) for part in split_three(turned))
    shifted = pltpu.roll(middle, WIDTH, axis=1)
    left = iota((8, LANES), 1) < WIDTH
    moments_ref[...] = jnp.where(left, top, shifted)
    rolled = pltpu.roll(rest, WIDTH, axis=1)
    low_half = iota((1, LANES), 1) < WIDTH
    for n in range(3):
        second = rolled[2 * n + 1 : 2 * n + 2, :]
        moments_ref[5 + n : 6 + n, :] = jnp.where(low_half, rest[2 * n : 2 * n + 1, :], second)


def unsort_kernel(x_ref, rank_ref, out_ref):
    for b in range(BLOCKS):
        out_ref[b] = unsort(x_ref[b], rank_ref[b : b + 1, :])


def two_sum(a, b):
    s = a + b
    back = s - a
    return s, (a - (s - back)) + (b - back)


def halves(a):
    scaled = 4097.0 * a
    top = scaled - (scaled - a)
    return top, a - top


def two_product(a, b):
    p = a * b
    a1, a2 = halves(a)
    b1, b2 = halves(b)
    return p, ((a1 * b1 - p) + a1 * b2 + a2 * b1) + a2 * b2


def pair_add(a, b):
    s, e = two_sum(a[0], b[0])
    return two_sum(s, e + (a[1] + b[1]))


def pair_mul(a, b):
    p, e = two_product(a[0], b[0])
    return two_sum(p, e + (a[0] * b[1] + a[1] * b[0]))


def final_kernel(moments_ref, start_ref, once_ref, twice_ref, solution_ref, residual_ref):
    gathered = moments_ref[...]
    rolled = pltpu.roll(gathered, WIDTH, axis=1)
    left = iota((1, LANES), 1) < WIDTH
    moments = []
    for n in range(5):
        source = gathered if n % 2 == 0 else rolled
        last = source[5 + n // 2 : 6 + n // 2, :]
        s, e = two_sum(gathered[n : n + 1, :], rolled[n : n + 1, :])
        s, e = two_sum(s, e + last)
        moments.append((jnp.where(left, s, 1.0), jnp.where(left, e, 0.0)))
    norm, curve, square, cross, cube = moments
    alpha = norm[0] / curve[0]
    step = (alpha, jnp.zeros_like(alpha))
    minus = (-alpha, jnp.zeros_like(alpha))
    step_sq = pair_mul(step, step)
    by_curve = pair_mul(minus, curve)
    norm_next = pair_add(pair_add(norm, pair_add(by_curve, by_curve)), pair_mul(step_sq, square))
    beta = norm_next[0] / norm[0]
    gamma = two_sum(jnp.ones_like(beta), beta)
    curve_next = pair_add(
        pair_mul(pair_mul(gamma, gamma), curve),
        pair_add(
            pair_mul(pair_mul(gamma, minus), pair_add(cross, square)),
            pair_mul(step_sq, cube),
        ),
    )
    alpha_next = norm_next[0] / curve_next[0]
    alpha, beta, alpha_next = (column(row)[0:WIDTH] for row in (alpha, beta, alpha_next))
    for o in range(BLOCKS):
        for ic in range(CHUNKS):
            at = (o, slice(None), lanes(ic))
            start, once, twice = start_ref[at], once_ref[at], twice_ref[at]
            residual = start - alpha * once
            direction = residual + beta * start
            image = (once - alpha * twice) + beta * once
            solution_ref[at] = alpha * start + alpha_next * direction
            residual_ref[at] = residual - alpha_next * image


def shape(*dims, dtype=F32):
    return jax.ShapeDtypeStruct(dims, dtype)


def call(kernel, out_shape, scratch=(), in_specs=None, count=None, flops=0, nbytes=1 << 20):
    outs = jax.tree.map(lambda _: VMEM, out_shape)
    return pl.pallas_call(
        kernel,
        out_shape=out_shape,
        in_specs=in_specs if in_specs is not None else [VMEM] * count,
        out_specs=outs,
        scratch_shapes=list(scratch),
        compiler_params=pltpu.CompilerParams(vmem_limit_bytes=LIMIT),
        cost_estimate=pl.CostEstimate(flops=flops, bytes_accessed=nbytes, transcendentals=0),
    )


def shift(x, axis, by):
    count = lax.axis_size(axis)
    return lax.ppermute(x, axis, [(i, i + by) for i in range(count) if 0 <= i + by < count])


SKY = ("z", "x", "core")


def sky_shift(x, by):
    count = lax.axis_size(SKY)
    return lax.ppermute(x, SKY, [(i, i + by) for i in range(count) if 0 <= i + by < count])


def with_halo(x):
    before, after = shift(x, "tm", 1), shift(x, "tm", -1)
    mid = jnp.concatenate([before, x, after], axis=0)
    return sky_shift(mid, 1), mid, sky_shift(mid, -1)


def local(star_pos, noise_var, targets, pair_list):
    ident = (lax.axis_index(SKY) * lax.axis_size("tm") + lax.axis_index("tm")) * BLOCKS
    block = shape(BLOCKS, WIDTH, STARS)
    pairs_scratch = [
        pltpu.VMEM((NEAR * CHUNKS, LANES, 2 * LANES), BF16),
        pltpu.VMEM((BLOCKS, 3, PADDED, LANES), F32),
        pltpu.VMEM((BLOCKS, PADDED, LANES), F32),
    ]
    packed, rank = call(
        sort_kernel,
        (shape(BLOCKS, ROWS, STARS), shape(BLOCKS, STARS)),
        scratch=[pltpu.VMEM((80, STARS), F32)],
        in_specs=[SMEM, VMEM, VMEM, VMEM, VMEM],
    )(ident.reshape(1), star_pos, noise_var, targets, pair_list)
    low, mid, high = with_halo(packed)
    once, places, table = call(
        first_kernel,
        (block, shape(NEAR * CHUNKS, 8, LANES), shape(TABLE_ROWS, LANES, dtype=jnp.int32)),
        scratch=pairs_scratch
        + [
            pltpu.VMEM((TABLE_ROWS, STARS), F32),
            pltpu.VMEM((TABLE_ROWS, LANES), F32),
            pltpu.VMEM((TABLE_ROWS, LANES), F32),
            pltpu.SMEM((TABLE_ROWS, LANES), jnp.int32),
            pltpu.SemaphoreType.DMA,
        ],
        count=3,
    )(low, mid, high)
    low, mid, high = with_halo(once)
    once_back = call(unsort_kernel, block, count=2)(once, rank)
    twice_back, moments = call(
        second_kernel,
        (block, shape(8, LANES)),
        scratch=pairs_scratch + [pltpu.VMEM((LANES, LANES), F32)],
        in_specs=[SMEM] + [VMEM] * 6,
    )(table, low, mid, high, places, packed, rank)
    moments = lax.psum(moments, ("x", "core"))
    moments = lax.psum(moments, "tm")
    moments = lax.psum(moments, "z")
    return call(final_kernel, (block, block), count=4)(moments, targets, once_back, twice_back)


def solution(mesh):
    sky, tm = mesh.devices.shape
    finer = Mesh(mesh.devices.reshape(sky // 8, 4, 2, tm), SKY + ("tm",))
    both = SKY + ("tm",)
    in_specs = (P(both, None, None), P(both, None), P(both, None, None), P(both, None))
    out_specs = (P(both, None, None), P(both, None, None))
    return jax.shard_map(local, mesh=finer, in_specs=in_specs, out_specs=out_specs, check_vma=False)
```

```python
import functools

import jax
import jax.numpy as jnp
from jax import lax
from jax.experimental import pallas as pl
from jax.experimental.pallas import tpu as pltpu
from jax.sharding import Mesh, PartitionSpec as P

F32 = jnp.float32
BF16 = jnp.bfloat16
BLOCKS, WIDTH, STARS, LANES = 2, 64, 512, 128
CHUNKS = STARS // LANES
NOISE, LIST, IDENT, META = 3, 4, 5, 8
COLUMNS = 16
ROWS = STARS + CHUNKS * BLOCKS * META
NEAR = 18
OWN = 8
LONG, SHORT = 256, 64
AT_ONCE = {LONG: 4, SHORT: 8}
KEPT = {LONG: 40, SHORT: 48}
PADDED = STARS + LONG
NOTHING = STARS
FIRST = {LONG: 8, SHORT: 320}
COUNT = {LONG: 0, SHORT: 1}
LISTS = 512
VMEM = pl.BlockSpec(memory_space=pltpu.VMEM)
SMEM = pl.BlockSpec(memory_space=pltpu.SMEM)
LIMIT = 32 * 1024 * 1024


def nt(left, right):
    return lax.dot_general(left, right, (((1,), (1,)), ((), ())), preferred_element_type=F32)


def nn(left, right):
    return lax.dot_general(left, right, (((1,), (0,)), ((), ())), preferred_element_type=F32)


def iota(shape, dim):
    return lax.broadcasted_iota(jnp.int32, shape, dim)


def column(row):
    return jnp.transpose(jnp.broadcast_to(row, (LANES, LANES)))


def lanes(chunk):
    return slice(chunk * LANES, (chunk + 1) * LANES)


def split_three(x):
    top = x.astype(BF16)
    rest = x - top.astype(F32)
    middle = rest.astype(BF16)
    return top, middle, (rest - middle.astype(F32)).astype(BF16)


def split_two(x):
    top = x.astype(BF16)
    return top, (x - top.astype(F32)).astype(BF16)


def one_hot(rank):
    same = iota((STARS, STARS), 0) == rank.astype(jnp.int32)
    return jnp.where(same, 1.0, 0.0).astype(BF16)


def fold(x):
    return x + pltpu.roll(x, WIDTH, axis=x.ndim - 1)


def left_half(rows):
    return iota((rows, LANES), 1) < WIDTH


def unsort(x, rank_ref, out_ref):
    turned = jnp.concatenate([jnp.transpose(x[lanes(jc), :]) for jc in range(CHUNKS)], axis=1)
    for b in range(BLOCKS):
        block = turned[b * WIDTH : (b + 1) * WIDTH]
        parts = nn(jnp.concatenate(split_three(block), axis=0), one_hot(rank_ref[b : b + 1, :]))
        out_ref[b] = (parts[:WIDTH] + parts[WIDTH : 2 * WIDTH]) + parts[2 * WIDTH :]


def ranks(times):
    counts = [jnp.zeros((1, LANES), F32) for _ in range(CHUNKS)]
    for jc in range(CHUNKS):
        other = column(times[:, lanes(jc)])
        for ic in range(CHUNKS):
            mine = times[:, lanes(ic)]
            if jc < ic:
                before = other <= mine
            elif jc > ic:
                before = other < mine
            else:
                earlier = iota((LANES, LANES), 0) < iota((LANES, LANES), 1)
                before = (other < mine) | ((other == mine) & earlier)
            counts[ic] += jnp.sum(jnp.where(before, 1.0, 0.0), axis=0, keepdims=True)
    return jnp.concatenate(counts, axis=1)


def meta_rows(b, jc):
    first = STARS + (jc * BLOCKS + b) * META
    return slice(first, first + META)


def sort_kernel(ident_ref, pos_ref, noise_ref, targets_ref, list_ref, packed_ref, rank_ref, tall, small):
    values = jnp.zeros((STARS, LANES), F32)
    for b in range(BLOCKS):
        rank = ranks(pos_ref[b, 2:3, :])
        rank_ref[b : b + 1, :] = rank
        where_to = one_hot(rank)
        tall[...] = jnp.zeros(tall.shape, F32)
        tall[b * WIDTH : (b + 1) * WIDTH, :] = targets_ref[b]
        parts = nt(where_to, jnp.concatenate(split_three(tall[...]), axis=0))
        values += (parts[:, lanes(0)] + parts[:, lanes(1)]) + parts[:, lanes(2)]
        small[...] = jnp.zeros(small.shape, F32)
        small[0:3, :] = pos_ref[b]
        small[NOISE : NOISE + 1, :] = noise_ref[b : b + 1, :]
        parts = nt(jnp.concatenate(split_three(small[...]), axis=0), where_to)
        height = small.shape[0]
        meta = ((parts[:height] + parts[height : 2 * height]) + parts[2 * height :])[0:META]
        for jc in range(CHUNKS):
            packed_ref[meta_rows(b, jc), :] = meta[:, lanes(jc)]
            first = STARS + (jc * BLOCKS + b) * META
            ident = jnp.full((1, LANES), (ident_ref[0] + b + 1).astype(F32))
            packed_ref[first + IDENT : first + IDENT + 1, :] = ident
        listed = list_ref[b : b + 1, :].astype(F32) + 1.0
        first = STARS + b * META + LIST
        packed_ref[first : first + 1, 0 : listed.shape[1]] = listed
    packed_ref[0:STARS, :] = values


def build_table(devices, own, chosen, table, times, lists, idents):
    rows = table.shape[0]
    for scratch in (times, lists, idents):
        scratch[...] = jnp.zeros(scratch.shape, F32)
    for d, device in enumerate(devices):
        for b in range(BLOCKS):
            k = BLOCKS * d + b
            for jc in range(CHUNKS):
                first = STARS + (jc * BLOCKS + b) * META
                times[k : k + 1, lanes(jc)] = device[first + 2 : first + 3, :]
            first = STARS + b * META
            lists[k : k + 1, :] = device[first + LIST : first + LIST + 1, :]
            idents[k : k + 1, :] = device[first + IDENT : first + IDENT + 1, :]
    place = iota((rows, LANES), 1)
    block = iota((rows, 1), 0)
    out = jnp.full((rows, LANES), -1, jnp.int32)
    ident = idents[:, 0:1]
    for o in range(BLOCKS):
        own_ident = idents[own + o : own + o + 1, 0:1]
        own_list = lists[own + o : own + o + 1, :]
        own_list = jnp.where(own_list == 0.0, -5.0, own_list)
        hit = jnp.where((lists[...] == own_ident) | (own_list == ident), 1.0, 0.0)
        linked = (jnp.max(hit, axis=1, keepdims=True) > 0.0) | (ident == own_ident)
        linked = linked & chosen(block)
        mine = times[own + o : own + o + 1, :]
        twice = jnp.zeros((rows, 1), jnp.int32)
        for jc in range(CHUNKS):
            first = times[:, jc * LANES : jc * LANES + 1]
            last = times[:, (jc + 1) * LANES - 1 : (jc + 1) * LANES]
            skipped = jnp.sum(jnp.where(first - mine >= 1.0, 1.0, 0.0), axis=1, keepdims=True)
            beyond = jnp.sum(jnp.where(mine - last >= 1.0, 1.0, 0.0), axis=1, keepdims=True)
            start = skipped.astype(jnp.int32)
            end = STARS - beyond.astype(jnp.int32)
            start = start - (start & 7)
            count = jnp.where(linked & (end > start), end - start, 0)
            whole = (count + (LONG - SHORT - 1)) // LONG
            twice = jnp.where(whole > 1, 1, twice)
            code = (block * CHUNKS + jc) * 2048 + (o * PADDED + start)
            steps = (
                jnp.where(whole > 0, code, -1),
                jnp.where(count > whole * LONG, code + whole * LONG, -1),
                jnp.where(whole > 1, code + LONG, -1),
            )
            for n, step in enumerate(steps):
                out = jnp.where(place == COLUMNS * o + n * CHUNKS + jc, step, out)
        flag = linked.astype(jnp.int32) + twice
        out = jnp.where(place == COLUMNS * o + 3 * CHUNKS, flag, out)
    table[...] = out


def list_steps(table, tasks, blocks):
    def per_block(k, counts):
        for o in range(BLOCKS):
            flag = table[k, COLUMNS * o + 3 * CHUNKS]

            def add(counts, o=o):
                counts = list(counts)
                for jc in range(CHUNKS):
                    for n, rows in enumerate((LONG, SHORT)):
                        code = table[k, COLUMNS * o + n * CHUNKS + jc]
                        tasks[FIRST[rows] + counts[n]] = code
                        counts[n] += (code >= 0).astype(jnp.int32)
                return tuple(counts)

            def more(counts, o=o):
                long, short = counts
                for jc in range(CHUNKS):
                    code = table[k, COLUMNS * o + 2 * CHUNKS + jc]
                    tasks[FIRST[LONG] + long] = code
                    long += (code >= 0).astype(jnp.int32)
                return long, short

            counts = lax.cond(flag > 0, add, lambda counts: counts, counts)
            counts = lax.cond(flag > 1, more, lambda counts: counts, counts)
        return counts

    counts = lax.fori_loop(0, blocks, per_block, (jnp.int32(0), jnp.int32(0)))
    for rows, count in zip((LONG, SHORT), counts):
        tasks[COUNT[rows]] = count
        for n in range(AT_ONCE[rows]):
            tasks[FIRST[rows] + count + n] = NOTHING


def stage_weights(device, d, weights):
    left = left_half(LANES)
    for jc in range(CHUNKS):
        x = device[lanes(jc), :]
        top = x.astype(BF16).astype(F32)
        rest = pltpu.roll(x - top, WIDTH, axis=1)
        weights[2 * d * CHUNKS + jc] = jnp.where(left, top, rest).astype(BF16)
        weights[(2 * d + 1) * CHUNKS + jc] = jnp.where(left, rest, top).astype(BF16)


def eval_tile(at, row, rows, own_pos, places, tile):
    step = 64
    for piece in range(rows // step):
        squared = None
        for c in range(3):
            mine = own_pos[c, pl.ds(row + piece * step, step), :]
            offset = mine - places[at, c : c + 1, :]
            squared = offset * offset if squared is None else squared + offset * offset
        radius = squared * lax.rsqrt(jnp.maximum(squared, 1e-30))
        margin = jnp.maximum(1.0 - radius, 0.0)
        margin_sq = margin * margin
        values = (margin_sq * margin_sq) * (1.2 * radius + 0.3)
        top, rest = split_two(values)
        tile[piece * step : (piece + 1) * step, 0:LANES] = top
        tile[piece * step : (piece + 1) * step, LANES:] = rest


def decode(code):
    return code >> 11, pl.multiple_of(code & 2047, 8)


def add_product(at, row, rows, tile, weights, total):
    both = jnp.concatenate([weights[at], weights[at]], axis=0)
    total[pl.ds(row, rows), :] += nn(tile, both)


def run_steps(tasks, own_pos, places, weights, total, tiles, skip=None):
    for rows in (LONG, SHORT):
        width = AT_ONCE[rows]
        begin = skip[rows] // width if skip else 0

        def some(i, _):
            picked = [decode(tasks[FIRST[rows] + width * i + n]) for n in range(width)]
            for n, (at, row) in enumerate(picked):
                eval_tile(at, row, rows, own_pos, places, tiles.at[n, 0:rows])
            for n, (at, row) in enumerate(picked):
                add_product(at, row, rows, tiles[n, 0:rows], weights, total)
            return 0

        lax.fori_loop(begin, (tasks[COUNT[rows]] + (width - 1)) // width, some, 0)


def keep_tiles(tasks, own_pos, places, kept):
    for rows in (LONG, SHORT):
        width = AT_ONCE[rows]

        def some(i, _):
            for n in range(width):
                at, row = decode(tasks[FIRST[rows] + width * i + n])
                eval_tile(at, row, rows, own_pos, places, kept[rows].at[width * i + n])
            return 0

        batches = (tasks[COUNT[rows]] + (width - 1)) // width
        lax.fori_loop(0, jnp.minimum(batches, KEPT[rows] // width), some, 0)


def run_kept(tasks, kept, weights, total):
    for rows in (LONG, SHORT):
        width = AT_ONCE[rows]

        def some(i, _):
            for n in range(width):
                at, row = decode(tasks[FIRST[rows] + width * i + n])
                add_product(at, row, rows, kept[rows][width * i + n], weights, total)
            return 0

        batches = (tasks[COUNT[rows]] + (width - 1)) // width
        lax.fori_loop(0, jnp.minimum(batches, KEPT[rows] // width), some, 0)


def own_rows(o):
    return slice(o * PADDED, o * PADDED + STARS)


def padding(o):
    return slice(o * PADDED + STARS, (o + 1) * PADDED)


def stage_own_sum(own_sum, total):
    for o in range(BLOCKS):
        total[own_rows(o), :] = own_sum[o * STARS : (o + 1) * STARS, :]
        total[padding(o), :] = jnp.zeros((PADDED - STARS, LANES), F32)


def image_of(total, own_pos, vector):
    left = left_half(STARS)
    noise = jnp.where(left, own_pos[NOISE, own_rows(0), :], own_pos[NOISE, own_rows(1), :])
    return noise * vector + jnp.where(left, fold(total[own_rows(0), :]), fold(total[own_rows(1), :]))


def stage_places(device, d, places):
    for b in range(BLOCKS):
        for jc in range(CHUNKS):
            places[(BLOCKS * d + b) * CHUNKS + jc] = device[meta_rows(b, jc), :]


def own_kernel(packed, own_pos, own_sum, places, own_tasks, weights, total, tiles, *scratch):
    times, lists, idents, table, scalars, sem = scratch
    build_table([packed], 0, lambda k: k < BLOCKS, table, times, lists, idents)
    copy = pltpu.make_async_copy(table, scalars, sem)
    copy.start()
    stage_places(packed, 0, places)
    stage_weights(packed, 0, weights)
    for o in range(BLOCKS):
        for c in range(NOISE + 1):
            for ic in range(CHUNKS):
                first = o * PADDED + ic * LANES
                own_pos[c, first : first + LANES, :] = column(places[o * CHUNKS + ic, c : c + 1, :])
            own_pos[c, padding(o), :] = jnp.zeros((PADDED - STARS, LANES), F32)
    total[...] = jnp.zeros(total.shape, F32)
    copy.wait()
    list_steps(scalars, own_tasks, BLOCKS)
    run_steps(own_tasks, own_pos, places, weights, total, tiles)
    for o in range(BLOCKS):
        own_sum[o * STARS : (o + 1) * STARS, :] = total[own_rows(o), :]


def first_kernel(
    low, mid, high, own_pos, own_sum, image_ref, places, tasks, weights, total, tiles, *scratch
):
    times, lists, idents, table, scalars, sem = scratch
    groups = (low, mid, high)
    devices = [groups[d // 3].at[d % 3] for d in range(9)]
    build_table(devices, OWN, lambda k: (k < OWN) | (k >= OWN + BLOCKS), table, times, lists, idents)
    copy = pltpu.make_async_copy(table, scalars, sem)
    copy.start()
    for d, device in enumerate(devices):
        if d != OWN // BLOCKS:
            stage_places(device, d, places)
            stage_weights(device, d, weights)
    stage_own_sum(own_sum, total)
    copy.wait()
    list_steps(scalars, tasks, NEAR)
    run_steps(tasks, own_pos, places, weights, total, tiles)
    image_ref[...] = image_of(total, own_pos, mid[1, 0:STARS, :])


def between_kernel(
    own_tasks, tasks, once, own_pos, own_places, places, own_sum, kept_long, kept_short, weights, total, tiles
):
    stage_weights(once, 0, weights)
    total[...] = jnp.zeros(total.shape, F32)
    run_steps(own_tasks, own_pos, own_places, weights, total, tiles)
    for o in range(BLOCKS):
        own_sum[o * STARS : (o + 1) * STARS, :] = total[own_rows(o), :]
    keep_tiles(tasks, own_pos, places, {LONG: kept_long, SHORT: kept_short})


def second_kernel(
    tasks,
    low,
    mid,
    high,
    own_pos,
    own_sum,
    places,
    kept_long,
    kept_short,
    packed,
    rank,
    image_ref,
    moments_ref,
    weights,
    total,
    tiles,
    sums,
):
    groups = (low, mid, high)
    for d in range(9):
        if d != OWN // BLOCKS:
            stage_weights(groups[d // 3].at[d % 3], d, weights)
    stage_own_sum(own_sum, total)
    run_kept(tasks, {LONG: kept_long, SHORT: kept_short}, weights, total)
    run_steps(tasks, own_pos, places, weights, total, tiles, skip=KEPT)
    start, once = packed[0:STARS, :], mid[1]
    twice = image_of(total, own_pos, once)
    products = (start * start, start * once, once * once, start * twice, once * twice)
    sums[...] = jnp.zeros(sums.shape, F32)
    for n, product in enumerate(products):
        sums[n : n + 1, :] = jnp.sum(product, axis=0, keepdims=True)
    top, middle, rest = (part.astype(F32) for part in split_three(fold(sums[...])))
    moments_ref[...] = jnp.where(left_half(8), top, middle)
    for n in range(3):
        pair = jnp.where(left_half(1), rest[2 * n : 2 * n + 1, :], rest[2 * n + 1 : 2 * n + 2, :])
        moments_ref[5 + n : 6 + n, :] = pair
    unsort(twice, rank, image_ref)


def unsort_kernel(x_ref, rank_ref, out_ref):
    unsort(x_ref[...], rank_ref, out_ref)


def two_sum(a, b):
    s = a + b
    back = s - a
    return s, (a - (s - back)) + (b - back)


def halves(a):
    scaled = 4097.0 * a
    top = scaled - (scaled - a)
    return top, a - top


def two_product(a, b):
    p = a * b
    a1, a2 = halves(a)
    b1, b2 = halves(b)
    return p, ((a1 * b1 - p) + a1 * b2 + a2 * b1) + a2 * b2


def pair_add(a, b):
    s, e = two_sum(a[0], b[0])
    return two_sum(s, e + (a[1] + b[1]))


def pair_mul(a, b):
    p, e = two_product(a[0], b[0])
    return two_sum(p, e + (a[0] * b[1] + a[1] * b[0]))


def final_kernel(moments_ref, start_ref, once_ref, twice_ref, solution_ref, residual_ref):
    gathered = moments_ref[...]
    rolled = pltpu.roll(gathered, WIDTH, axis=1)
    left = iota((1, LANES), 1) < WIDTH
    moments = []
    for n in range(5):
        source = gathered if n % 2 == 0 else rolled
        last = source[5 + n // 2 : 6 + n // 2, :]
        s, e = two_sum(gathered[n : n + 1, :], rolled[n : n + 1, :])
        s, e = two_sum(s, e + last)
        moments.append((jnp.where(left, s, 1.0), jnp.where(left, e, 0.0)))
    norm, curve, square, cross, cube = moments
    alpha = norm[0] / curve[0]
    step = (alpha, jnp.zeros_like(alpha))
    minus = (-alpha, jnp.zeros_like(alpha))
    step_sq = pair_mul(step, step)
    by_curve = pair_mul(minus, curve)
    norm_next = pair_add(pair_add(norm, pair_add(by_curve, by_curve)), pair_mul(step_sq, square))
    beta = norm_next[0] / norm[0]
    gamma = two_sum(jnp.ones_like(beta), beta)
    curve_next = pair_add(
        pair_mul(pair_mul(gamma, gamma), curve),
        pair_add(
            pair_mul(pair_mul(gamma, minus), pair_add(cross, square)),
            pair_mul(step_sq, cube),
        ),
    )
    alpha_next = norm_next[0] / curve_next[0]
    alpha, beta, alpha_next = (column(row)[0:WIDTH] for row in (alpha, beta, alpha_next))
    for o in range(BLOCKS):
        for ic in range(CHUNKS):
            at = (o, slice(None), lanes(ic))
            start, once, twice = start_ref[at], once_ref[at], twice_ref[at]
            residual = start - alpha * once
            direction = residual + beta * start
            image = (once - alpha * twice) + beta * once
            solution_ref[at] = alpha * start + alpha_next * direction
            residual_ref[at] = residual - alpha_next * image


def shape(*dims, dtype=F32):
    return jax.ShapeDtypeStruct(dims, dtype)


def call(kernel, out_shape, scratch=(), in_specs=None, count=None, out_specs=None, flops=0, nbytes=1 << 20):
    return pl.pallas_call(
        kernel,
        out_shape=out_shape,
        in_specs=in_specs if in_specs is not None else [VMEM] * count,
        out_specs=out_specs or jax.tree.map(lambda _: VMEM, out_shape),
        scratch_shapes=list(scratch),
        compiler_params=pltpu.CompilerParams(vmem_limit_bytes=LIMIT),
        cost_estimate=pl.CostEstimate(flops=flops, bytes_accessed=nbytes, transcendentals=0),
    )


BLOCK = shape(BLOCKS, WIDTH, STARS)
OWN_POS = shape(NOISE + 1, BLOCKS * PADDED, LANES)
OWN_SUM = shape(BLOCKS * STARS, LANES)
TASKS = shape(LISTS, dtype=jnp.int32)


def pairs_scratch(blocks):
    return [
        pltpu.VMEM((blocks * CHUNKS, LANES, LANES), BF16),
        pltpu.VMEM((BLOCKS * PADDED, LANES), F32),
        pltpu.VMEM((max(AT_ONCE.values()), LONG, 2 * LANES), BF16),
    ]


def table_scratch(rows):
    return [
        pltpu.VMEM((rows, STARS), F32),
        pltpu.VMEM((rows, LANES), F32),
        pltpu.VMEM((rows, LANES), F32),
        pltpu.VMEM((rows, LANES), jnp.int32),
        pltpu.SMEM((rows, LANES), jnp.int32),
        pltpu.SemaphoreType.DMA,
    ]


def apply_own(packed):
    return call(
        own_kernel,
        (OWN_POS, OWN_SUM, shape(BLOCKS * CHUNKS, META, LANES), TASKS),
        scratch=pairs_scratch(BLOCKS) + table_scratch(8),
        count=1,
        out_specs=(VMEM, VMEM, VMEM, SMEM),
        flops=1 << 30,
    )(packed)


def apply_first(low, mid, high, own_pos, own_sum):
    return call(
        first_kernel,
        (shape(STARS, LANES), shape(NEAR * CHUNKS, META, LANES), TASKS),
        scratch=pairs_scratch(NEAR) + table_scratch(24),
        count=5,
        out_specs=(VMEM, VMEM, SMEM),
    )(low, mid, high, own_pos, own_sum)


def apply_between(own_tasks, tasks, once, own_pos, own_places, places):
    return call(
        between_kernel,
        (
            OWN_SUM,
            shape(KEPT[LONG], LONG, 2 * LANES, dtype=BF16),
            shape(KEPT[SHORT], SHORT, 2 * LANES, dtype=BF16),
        ),
        scratch=pairs_scratch(BLOCKS),
        in_specs=[SMEM, SMEM] + [VMEM] * 4,
        flops=1 << 30,
    )(own_tasks, tasks, once, own_pos, own_places, places)


def apply_second(tasks, low, mid, high, own_pos, own_sum, places, kept_long, kept_short, packed, rank):
    return call(
        second_kernel,
        (BLOCK, shape(8, LANES)),
        scratch=pairs_scratch(NEAR) + [pltpu.VMEM((8, LANES), F32)],
        in_specs=[SMEM] + [VMEM] * 10,
    )(tasks, low, mid, high, own_pos, own_sum, places, kept_long, kept_short, packed, rank)


def shift(x, axis, by):
    count = lax.axis_size(axis)
    return lax.ppermute(x, axis, [(i, i + by) for i in range(count) if 0 <= i + by < count])


SKY = ("far", "near", "x", "core")


def sky_shift(x, by):
    count = lax.axis_size(SKY)
    return lax.ppermute(x, SKY, [(i, i + by) for i in range(count) if 0 <= i + by < count])


def with_halo(x):
    before, after = shift(x, "tm", 1), shift(x, "tm", -1)
    mid = jnp.stack([before, x, after])
    return sky_shift(mid, 1), mid, sky_shift(mid, -1)


def local(star_pos, noise_var, targets, pair_list):
    ident = (lax.axis_index(SKY) * lax.axis_size("tm") + lax.axis_index("tm")) * BLOCKS
    packed, rank = call(
        sort_kernel,
        (shape(ROWS, LANES), shape(BLOCKS, STARS)),
        scratch=[pltpu.VMEM((BLOCKS * WIDTH, STARS), F32), pltpu.VMEM((2 * META, STARS), F32)],
        in_specs=[SMEM, VMEM, VMEM, VMEM, VMEM],
    )(ident.reshape(1), star_pos, noise_var, targets, pair_list)
    low, mid, high = with_halo(packed)
    own_pos, own_sum, own_places, own_tasks = apply_own(packed)
    once, places, tasks = apply_first(low, mid, high, own_pos, own_sum)
    low, mid, high = with_halo(once)
    own_sum, *kept = apply_between(own_tasks, tasks, once, own_pos, own_places, places)
    once_back = call(unsort_kernel, BLOCK, count=2, flops=1 << 28)(once, rank)
    twice_back, moments = apply_second(
        tasks, low, mid, high, own_pos, own_sum, places, *kept, packed, rank
    )
    for axis in ("core", "x", "tm", "near", "far"):
        moments = lax.psum(moments, axis)
    return call(final_kernel, (BLOCK, BLOCK), count=4)(moments, targets, once_back, twice_back)


def solution(mesh):
    sky, tm = mesh.devices.shape
    near = 4 if sky % 32 == 0 else 1
    finer = Mesh(mesh.devices.reshape(sky // (8 * near), near, 4, 2, tm), SKY + ("tm",))
    both = SKY + ("tm",)
    in_specs = (P(both, None, None), P(both, None), P(both, None, None), P(both, None))
    out_specs = (P(both, None, None), P(both, None, None))
    return jax.shard_map(local, mesh=finer, in_specs=in_specs, out_specs=out_specs, check_vma=False)
```

```python
import functools

import jax
import jax.numpy as jnp
from jax import lax
from jax.experimental import pallas as pl
from jax.experimental.pallas import tpu as pltpu
from jax.sharding import Mesh, PartitionSpec as P

F32 = jnp.float32
BF16 = jnp.bfloat16
BLOCKS, WIDTH, STARS, LANES = 2, 64, 512, 128
CHUNKS = STARS // LANES
NOISE, LIST, IDENT, META = 3, 4, 5, 8
SLOTS = 16
ROWS = STARS + CHUNKS * BLOCKS * META
NEAR = 18
OWN = 8
LONG, SHORT = 256, 64
AT_ONCE = {LONG: 4, SHORT: 8}
KEPT = {LONG: 40, SHORT: 48}
PADDED = STARS + LONG
NOTHING = STARS
FIRST = {LONG: 8, SHORT: 320}
COUNT = {LONG: 0, SHORT: 1}
LISTS = 512
VMEM = pl.BlockSpec(memory_space=pltpu.VMEM)
SMEM = pl.BlockSpec(memory_space=pltpu.SMEM)
LIMIT = 32 * 1024 * 1024


def nt(left, right):
    return lax.dot_general(left, right, (((1,), (1,)), ((), ())), preferred_element_type=F32)


def nn(left, right):
    return lax.dot_general(left, right, (((1,), (0,)), ((), ())), preferred_element_type=F32)


def iota(shape, dim):
    return lax.broadcasted_iota(jnp.int32, shape, dim)


def column(row):
    return jnp.transpose(jnp.broadcast_to(row, (LANES, LANES)))


def lanes(chunk):
    return slice(chunk * LANES, (chunk + 1) * LANES)


def split_three(x):
    top = x.astype(BF16)
    rest = x - top.astype(F32)
    middle = rest.astype(BF16)
    return top, middle, (rest - middle.astype(F32)).astype(BF16)


def split_two(x):
    top = x.astype(BF16)
    return top, (x - top.astype(F32)).astype(BF16)


def one_hot(rank):
    same = iota((STARS, STARS), 0) == rank.astype(jnp.int32)
    return jnp.where(same, 1.0, 0.0).astype(BF16)


def fold(x):
    return x + pltpu.roll(x, WIDTH, axis=x.ndim - 1)


def left_half(rows):
    return iota((rows, LANES), 1) < WIDTH


def unsort(x, rank_ref, out_ref):
    turned = jnp.concatenate([jnp.transpose(x[lanes(jc), :]) for jc in range(CHUNKS)], axis=1)
    for b in range(BLOCKS):
        block = turned[b * WIDTH : (b + 1) * WIDTH]
        parts = nn(jnp.concatenate(split_three(block), axis=0), one_hot(rank_ref[b : b + 1, :]))
        out_ref[b] = (parts[:WIDTH] + parts[WIDTH : 2 * WIDTH]) + parts[2 * WIDTH :]


def ranks(times):
    counts = [jnp.zeros((1, LANES), F32) for _ in range(CHUNKS)]
    for jc in range(CHUNKS):
        other = column(times[:, lanes(jc)])
        for ic in range(CHUNKS):
            mine = times[:, lanes(ic)]
            if jc < ic:
                before = other <= mine
            elif jc > ic:
                before = other < mine
            else:
                earlier = iota((LANES, LANES), 0) < iota((LANES, LANES), 1)
                before = (other < mine) | ((other == mine) & earlier)
            counts[ic] += jnp.sum(jnp.where(before, 1.0, 0.0), axis=0, keepdims=True)
    return jnp.concatenate(counts, axis=1)


def meta_rows(b, jc):
    first = STARS + (jc * BLOCKS + b) * META
    return slice(first, first + META)


def sort_kernel(ident_ref, pos_ref, noise_ref, targets_ref, list_ref, packed_ref, rank_ref, tall, small):
    values = jnp.zeros((STARS, LANES), F32)
    for b in range(BLOCKS):
        rank = ranks(pos_ref[2, b : b + 1, :])
        rank_ref[b : b + 1, :] = rank
        where_to = one_hot(rank)
        tall[...] = jnp.zeros(tall.shape, F32)
        tall[b * WIDTH : (b + 1) * WIDTH, :] = targets_ref[b]
        parts = nt(where_to, jnp.concatenate(split_three(tall[...]), axis=0))
        values += (parts[:, lanes(0)] + parts[:, lanes(1)]) + parts[:, lanes(2)]
        small[...] = jnp.zeros(small.shape, F32)
        for c in range(3):
            small[c : c + 1, :] = pos_ref[c, b : b + 1, :]
        small[NOISE : NOISE + 1, :] = noise_ref[b : b + 1, :]
        parts = nt(jnp.concatenate(split_three(small[...]), axis=0), where_to)
        height = small.shape[0]
        meta = ((parts[:height] + parts[height : 2 * height]) + parts[2 * height :])[0:META]
        listed = list_ref[b : b + 1, :].astype(F32) + 1.0
        for jc in range(CHUNKS):
            packed_ref[meta_rows(b, jc), :] = meta[:, lanes(jc)]
            first = STARS + (jc * BLOCKS + b) * META
            ident = jnp.full((1, LANES), (ident_ref[0] + b + 1).astype(F32))
            packed_ref[first + IDENT : first + IDENT + 1, :] = ident
            packed_ref[first + LIST : first + LIST + 1, 0 : listed.shape[1]] = listed
    packed_ref[0:STARS, :] = values


def build_table(places, blocks, own, own_times, chosen, table, turned):
    entries = blocks * CHUNKS
    turned[...] = jnp.zeros(turned.shape, F32)
    flipped = []
    for n, row in enumerate((2, LIST, IDENT)):
        for at in range(entries):
            turned[n, at : at + 1, :] = places[at, row : row + 1, :]
        flipped.append(jnp.transpose(turned[n]))
    times, lists, idents = flipped
    first, last = times[0:1, :], times[LANES - 1 : LANES, :]
    lists, ident = lists[0:SLOTS, :], idents[0:1, :]
    entry = iota((1, LANES), 1)
    rows = []
    for o in range(BLOCKS):
        at = (own + o) * CHUNKS
        own_ident = turned[2, at : at + 1, :]
        own_list = jnp.where(lists == 0.0, -5.0, lists)[:, at : at + 1]
        hit = jnp.where((lists == own_ident) | (own_list == ident), 1.0, 0.0)
        linked = (jnp.max(hit, axis=0, keepdims=True) > 0.0) | (ident == own_ident)
        linked = linked & chosen(entry) & (entry < entries)
        mine = own_times(o)
        skipped = jnp.sum(jnp.where(first - mine >= 1.0, 1.0, 0.0), axis=0, keepdims=True)
        beyond = jnp.sum(jnp.where(mine - last >= 1.0, 1.0, 0.0), axis=0, keepdims=True)
        start = skipped.astype(jnp.int32)
        end = STARS - beyond.astype(jnp.int32)
        start = start - (start & 7)
        count = jnp.where(linked & (end > start), end - start, 0)
        whole = (count + (LONG - SHORT - 1)) // LONG
        code = entry * 2048 + (o * PADDED + start)
        rows += [
            jnp.where(whole > 0, code, -1),
            jnp.where(count > whole * LONG, code + whole * LONG, -1),
            jnp.where(whole > 1, code + LONG, -1),
            jnp.where(whole > 1, 2, jnp.where(linked, 1, 0)),
        ]
    for n, row in enumerate(rows):
        table[n : n + 1, :] = row


def list_steps(table, tasks, blocks):
    def per_block(k, counts):
        for o in range(BLOCKS):
            flags = [table[4 * o + 3, CHUNKS * k + jc] for jc in range(CHUNKS)]

            def add(counts, o=o):
                counts = list(counts)
                codes = [[table[4 * o + n, CHUNKS * k + jc] for jc in range(CHUNKS)] for n in range(2)]
                for jc in range(CHUNKS):
                    for n, rows in enumerate((LONG, SHORT)):
                        tasks[FIRST[rows] + counts[n]] = codes[n][jc]
                        counts[n] += (codes[n][jc] >= 0).astype(jnp.int32)
                return tuple(counts)

            def more(counts, o=o):
                long, short = counts
                for jc in range(CHUNKS):
                    code = table[4 * o + 2, CHUNKS * k + jc]
                    tasks[FIRST[LONG] + long] = code
                    long += (code >= 0).astype(jnp.int32)
                return long, short

            counts = lax.cond(flags[0] > 0, add, lambda counts: counts, counts)
            most = jnp.maximum(jnp.maximum(flags[0], flags[1]), jnp.maximum(flags[2], flags[3]))
            counts = lax.cond(most > 1, more, lambda counts: counts, counts)
        return counts

    counts = lax.fori_loop(0, blocks, per_block, (jnp.int32(0), jnp.int32(0)))
    for rows, count in zip((LONG, SHORT), counts):
        tasks[COUNT[rows]] = count
        for n in range(AT_ONCE[rows]):
            tasks[FIRST[rows] + count + n] = NOTHING


def stage_weights(device, d, weights):
    left = left_half(LANES)
    for jc in range(CHUNKS):
        x = device[lanes(jc), :]
        top = x.astype(BF16).astype(F32)
        rest = pltpu.roll(x - top, WIDTH, axis=1)
        weights[2 * d * CHUNKS + jc] = jnp.where(left, top, rest).astype(BF16)
        weights[(2 * d + 1) * CHUNKS + jc] = jnp.where(left, rest, top).astype(BF16)


def eval_tile(at, row, rows, own_pos, places, tile):
    step = 64
    for piece in range(rows // step):
        squared = None
        for c in range(3):
            mine = own_pos[c, pl.ds(row + piece * step, step), :]
            offset = mine - places[at, c : c + 1, :]
            squared = offset * offset if squared is None else squared + offset * offset
        radius = squared * lax.rsqrt(jnp.maximum(squared, 1e-30))
        margin = jnp.maximum(1.0 - radius, 0.0)
        margin_sq = margin * margin
        values = (margin_sq * margin_sq) * (1.2 * radius + 0.3)
        top, rest = split_two(values)
        tile[piece * step : (piece + 1) * step, 0:LANES] = top
        tile[piece * step : (piece + 1) * step, LANES:] = rest


def decode(code):
    return code >> 11, pl.multiple_of(code & 2047, 8)


def add_product(at, row, rows, tile, weights, total):
    both = jnp.concatenate([weights[at], weights[at]], axis=0)
    total[pl.ds(row, rows), :] += nn(tile, both)


def run_steps(tasks, own_pos, places, weights, total, tiles, skip=None):
    for rows in (LONG, SHORT):
        width = AT_ONCE[rows]
        begin = skip[rows] // width if skip else 0

        def some(i, _):
            picked = [decode(tasks[FIRST[rows] + width * i + n]) for n in range(width)]
            for n in range(width + 1):
                if n < width:
                    at, row = picked[n]
                    eval_tile(at, row, rows, own_pos, places, tiles.at[n, 0:rows])
                if n > 0:
                    at, row = picked[n - 1]
                    add_product(at, row, rows, tiles[n - 1, 0:rows], weights, total)
            return 0

        lax.fori_loop(begin, (tasks[COUNT[rows]] + (width - 1)) // width, some, 0)


def keep_tiles(tasks, own_pos, places, kept):
    for rows in (LONG, SHORT):
        width = AT_ONCE[rows]

        def some(i, _):
            for n in range(width):
                at, row = decode(tasks[FIRST[rows] + width * i + n])
                eval_tile(at, row, rows, own_pos, places, kept[rows].at[width * i + n])
            return 0

        batches = (tasks[COUNT[rows]] + (width - 1)) // width
        lax.fori_loop(0, jnp.minimum(batches, KEPT[rows] // width), some, 0)


def run_kept(tasks, kept, weights, total):
    for rows in (LONG, SHORT):
        width = AT_ONCE[rows]

        def some(i, _):
            for n in range(width):
                at, row = decode(tasks[FIRST[rows] + width * i + n])
                add_product(at, row, rows, kept[rows][width * i + n], weights, total)
            return 0

        batches = (tasks[COUNT[rows]] + (width - 1)) // width
        lax.fori_loop(0, jnp.minimum(batches, KEPT[rows] // width), some, 0)


def own_rows(o):
    return slice(o * PADDED, o * PADDED + STARS)


def padding(o):
    return slice(o * PADDED + STARS, (o + 1) * PADDED)


def stage_own_sum(own_sum, total):
    for o in range(BLOCKS):
        total[own_rows(o), :] = own_sum[o * STARS : (o + 1) * STARS, :]
        total[padding(o), :] = jnp.zeros((PADDED - STARS, LANES), F32)


def image_of(total, own_pos, vector):
    left = left_half(STARS)
    noise = jnp.where(left, own_pos[NOISE, own_rows(0), :], own_pos[NOISE, own_rows(1), :])
    return noise * vector + jnp.where(left, fold(total[own_rows(0), :]), fold(total[own_rows(1), :]))


def stage_places(device, d, places):
    for b in range(BLOCKS):
        for jc in range(CHUNKS):
            places[(BLOCKS * d + b) * CHUNKS + jc] = device[meta_rows(b, jc), :]


def own_kernel(packed, own_pos, own_sum, places, own_tasks, weights, total, tiles, *scratch):
    turned, table, scalars, sem = scratch
    stage_places(packed, 0, places)
    for o in range(BLOCKS):
        for c in range(NOISE + 1):
            for ic in range(CHUNKS):
                first = o * PADDED + ic * LANES
                own_pos[c, first : first + LANES, :] = column(places[o * CHUNKS + ic, c : c + 1, :])
            own_pos[c, padding(o), :] = jnp.zeros((PADDED - STARS, LANES), F32)
    build_table(places, BLOCKS, 0, lambda o: own_pos[2, own_rows(o), :], lambda e: e >= 0, table, turned)
    copy = pltpu.make_async_copy(table, scalars, sem)
    copy.start()
    stage_weights(packed, 0, weights)
    total[...] = jnp.zeros(total.shape, F32)
    copy.wait()
    list_steps(scalars, own_tasks, BLOCKS)
    run_steps(own_tasks, own_pos, places, weights, total, tiles)
    for o in range(BLOCKS):
        own_sum[o * STARS : (o + 1) * STARS, :] = total[own_rows(o), :]


def first_kernel(
    low_pair,
    low,
    mid_pair,
    high_pair,
    high,
    own,
    own_pos,
    own_sum,
    image_ref,
    places,
    tasks,
    weights,
    total,
    tiles,
    *scratch,
):
    turned, table, scalars, sem = scratch
    devices = nine(low_pair, low, mid_pair, high_pair, high, own)
    for d, device in enumerate(devices):
        stage_places(device, d, places)

    def others(entry):
        return (entry < OWN * CHUNKS) | (entry >= (OWN + BLOCKS) * CHUNKS)

    build_table(places, NEAR, OWN, lambda o: own_pos[2, own_rows(o), :], others, table, turned)
    copy = pltpu.make_async_copy(table, scalars, sem)
    copy.start()
    for d, device in enumerate(devices):
        if d != OWN // BLOCKS:
            stage_weights(device, d, weights)
    stage_own_sum(own_sum, total)
    copy.wait()
    list_steps(scalars, tasks, NEAR)
    run_steps(tasks, own_pos, places, weights, total, tiles)
    image_ref[...] = image_of(total, own_pos, own[0:STARS, :])


def between_kernel(
    own_tasks, tasks, once, own_pos, own_places, places, own_sum, kept_long, kept_short, weights, total, tiles
):
    stage_weights(once, 0, weights)
    total[...] = jnp.zeros(total.shape, F32)
    run_steps(own_tasks, own_pos, own_places, weights, total, tiles)
    for o in range(BLOCKS):
        own_sum[o * STARS : (o + 1) * STARS, :] = total[own_rows(o), :]
    keep_tiles(tasks, own_pos, places, {LONG: kept_long, SHORT: kept_short})


def second_kernel(
    tasks,
    low_pair,
    low,
    mid_pair,
    high_pair,
    high,
    once,
    own_pos,
    own_sum,
    places,
    kept_long,
    kept_short,
    packed,
    rank,
    image_ref,
    moments_ref,
    weights,
    total,
    tiles,
    sums,
):
    for d, device in enumerate(nine(low_pair, low, mid_pair, high_pair, high, once)):
        if d != OWN // BLOCKS:
            stage_weights(device, d, weights)
    stage_own_sum(own_sum, total)
    run_kept(tasks, {LONG: kept_long, SHORT: kept_short}, weights, total)
    run_steps(tasks, own_pos, places, weights, total, tiles, skip=KEPT)
    start, once = packed[0:STARS, :], once[...]
    twice = image_of(total, own_pos, once)
    products = (start * start, start * once, once * once, start * twice, once * twice)
    sums[...] = jnp.zeros(sums.shape, F32)
    for n, product in enumerate(products):
        sums[n : n + 1, :] = jnp.sum(product, axis=0, keepdims=True)
    top, middle, rest = (part.astype(F32) for part in split_three(fold(sums[...])))
    moments_ref[...] = jnp.where(left_half(8), top, middle)
    for n in range(3):
        pair = jnp.where(left_half(1), rest[2 * n : 2 * n + 1, :], rest[2 * n + 1 : 2 * n + 2, :])
        moments_ref[5 + n : 6 + n, :] = pair
    unsort(twice, rank, image_ref)


def unsort_kernel(x_ref, rank_ref, out_ref):
    unsort(x_ref[...], rank_ref, out_ref)


def two_sum(a, b):
    s = a + b
    back = s - a
    return s, (a - (s - back)) + (b - back)


def halves(a):
    scaled = 4097.0 * a
    top = scaled - (scaled - a)
    return top, a - top


def two_product(a, b):
    p = a * b
    a1, a2 = halves(a)
    b1, b2 = halves(b)
    return p, ((a1 * b1 - p) + a1 * b2 + a2 * b1) + a2 * b2


def pair_add(a, b):
    s, e = two_sum(a[0], b[0])
    return two_sum(s, e + (a[1] + b[1]))


def pair_mul(a, b):
    p, e = two_product(a[0], b[0])
    return two_sum(p, e + (a[0] * b[1] + a[1] * b[0]))


def final_kernel(moments_ref, start_ref, once_ref, twice_ref, solution_ref, residual_ref):
    gathered = moments_ref[...]
    rolled = pltpu.roll(gathered, WIDTH, axis=1)
    left = iota((1, LANES), 1) < WIDTH
    moments = []
    for n in range(5):
        source = gathered if n % 2 == 0 else rolled
        last = source[5 + n // 2 : 6 + n // 2, :]
        s, e = two_sum(gathered[n : n + 1, :], rolled[n : n + 1, :])
        s, e = two_sum(s, e + last)
        moments.append((jnp.where(left, s, 1.0), jnp.where(left, e, 0.0)))
    norm, curve, square, cross, cube = moments
    alpha = norm[0] / curve[0]
    step = (alpha, jnp.zeros_like(alpha))
    minus = (-alpha, jnp.zeros_like(alpha))
    step_sq = pair_mul(step, step)
    by_curve = pair_mul(minus, curve)
    norm_next = pair_add(pair_add(norm, pair_add(by_curve, by_curve)), pair_mul(step_sq, square))
    beta = norm_next[0] / norm[0]
    gamma = two_sum(jnp.ones_like(beta), beta)
    curve_next = pair_add(
        pair_mul(pair_mul(gamma, gamma), curve),
        pair_add(
            pair_mul(pair_mul(gamma, minus), pair_add(cross, square)),
            pair_mul(step_sq, cube),
        ),
    )
    alpha_next = norm_next[0] / curve_next[0]
    alpha, beta, alpha_next = (column(row)[0:WIDTH] for row in (alpha, beta, alpha_next))
    for o in range(BLOCKS):
        for ic in range(CHUNKS):
            at = (o, slice(None), lanes(ic))
            start, once, twice = start_ref[at], once_ref[at], twice_ref[at]
            residual = start - alpha * once
            direction = residual + beta * start
            image = (once - alpha * twice) + beta * once
            solution_ref[at] = alpha * start + alpha_next * direction
            residual_ref[at] = residual - alpha_next * image


def shape(*dims, dtype=F32):
    return jax.ShapeDtypeStruct(dims, dtype)


def call(kernel, out_shape, scratch=(), in_specs=None, count=None, out_specs=None, flops=0, nbytes=1 << 20):
    return pl.pallas_call(
        kernel,
        out_shape=out_shape,
        in_specs=in_specs if in_specs is not None else [VMEM] * count,
        out_specs=out_specs or jax.tree.map(lambda _: VMEM, out_shape),
        scratch_shapes=list(scratch),
        compiler_params=pltpu.CompilerParams(vmem_limit_bytes=LIMIT),
        cost_estimate=pl.CostEstimate(flops=flops, bytes_accessed=nbytes, transcendentals=0),
    )


BLOCK = shape(BLOCKS, WIDTH, STARS)
OWN_POS = shape(NOISE + 1, BLOCKS * PADDED, LANES)
OWN_SUM = shape(BLOCKS * STARS, LANES)
TASKS = shape(LISTS, dtype=jnp.int32)


def pairs_scratch(blocks):
    return [
        pltpu.VMEM((blocks * CHUNKS, LANES, LANES), BF16),
        pltpu.VMEM((BLOCKS * PADDED, LANES), F32),
        pltpu.VMEM((max(AT_ONCE.values()), LONG, 2 * LANES), BF16),
    ]


TABLE_SCRATCH = [
    pltpu.VMEM((3, LANES, LANES), F32),
    pltpu.VMEM((8, LANES), jnp.int32),
    pltpu.SMEM((8, LANES), jnp.int32),
    pltpu.SemaphoreType.DMA,
]


def apply_own(packed):
    return call(
        own_kernel,
        (OWN_POS, OWN_SUM, shape(BLOCKS * CHUNKS, META, LANES), TASKS),
        scratch=pairs_scratch(BLOCKS) + TABLE_SCRATCH,
        count=1,
        out_specs=(VMEM, VMEM, VMEM, SMEM),
        flops=1 << 30,
    )(packed)


def apply_first(near, own, own_pos, own_sum):
    return call(
        first_kernel,
        (shape(STARS, LANES), shape(NEAR * CHUNKS, META, LANES), TASKS),
        scratch=pairs_scratch(NEAR) + TABLE_SCRATCH,
        count=8,
        out_specs=(VMEM, VMEM, SMEM),
    )(*near, own, own_pos, own_sum)


def apply_between(own_tasks, tasks, once, own_pos, own_places, places):
    return call(
        between_kernel,
        (
            OWN_SUM,
            shape(KEPT[LONG], LONG, 2 * LANES, dtype=BF16),
            shape(KEPT[SHORT], SHORT, 2 * LANES, dtype=BF16),
        ),
        scratch=pairs_scratch(BLOCKS),
        in_specs=[SMEM, SMEM] + [VMEM] * 4,
        flops=1 << 30,
    )(own_tasks, tasks, once, own_pos, own_places, places)


def apply_second(tasks, near, once, own_pos, own_sum, places, kept_long, kept_short, packed, rank):
    return call(
        second_kernel,
        (BLOCK, shape(8, LANES)),
        scratch=pairs_scratch(NEAR) + [pltpu.VMEM((8, LANES), F32)],
        in_specs=[SMEM] + [VMEM] * 13,
    )(tasks, *near, once, own_pos, own_sum, places, kept_long, kept_short, packed, rank)


def shift(x, axis, by):
    count = lax.axis_size(axis)
    return lax.ppermute(x, axis, [(i, i + by) for i in range(count) if 0 <= i + by < count])


SKY = ("far", "near", "x", "core")


def sky_shift(x, by):
    count = lax.axis_size(SKY)
    return lax.ppermute(x, SKY, [(i, i + by) for i in range(count) if 0 <= i + by < count])


def with_halo(x):
    beside = shift(x, "tm", 1), shift(x, "tm", -1), sky_shift(x, 1), sky_shift(x, -1)
    before, after, low, high = lax.optimization_barrier(beside)
    mid = jnp.stack([before, after])
    return sky_shift(mid, 1), low, mid, sky_shift(mid, -1), high


def nine(low_pair, low, mid_pair, high_pair, high, own):
    return [
        low_pair.at[0],
        low,
        low_pair.at[1],
        mid_pair.at[0],
        own,
        mid_pair.at[1],
        high_pair.at[0],
        high,
        high_pair.at[1],
    ]


def local(star_pos, noise_var, targets, pair_list):
    ident = (lax.axis_index(SKY) * lax.axis_size("tm") + lax.axis_index("tm")) * BLOCKS
    packed, rank = call(
        sort_kernel,
        (shape(ROWS, LANES), shape(BLOCKS, STARS)),
        scratch=[pltpu.VMEM((BLOCKS * WIDTH, STARS), F32), pltpu.VMEM((2 * META, STARS), F32)],
        in_specs=[SMEM, VMEM, VMEM, VMEM, VMEM],
    )(ident.reshape(1), jnp.swapaxes(star_pos, 0, 1), noise_var, targets, pair_list)
    near = with_halo(packed)
    own_pos, own_sum, own_places, own_tasks = apply_own(packed)
    once, places, tasks = apply_first(near, packed, own_pos, own_sum)
    near = with_halo(once)
    own_sum, *kept = apply_between(own_tasks, tasks, once, own_pos, own_places, places)
    once_back = call(unsort_kernel, BLOCK, count=2, flops=1 << 28)(once, rank)
    twice_back, moments = apply_second(
        tasks, near, once, own_pos, own_sum, places, *kept, packed, rank
    )
    for axis in ("core", "x", "tm", "near", "far"):
        moments = lax.psum(moments, axis)
    return call(final_kernel, (BLOCK, BLOCK), count=4)(moments, targets, once_back, twice_back)


def solution(mesh):
    sky, tm = mesh.devices.shape
    near = 4 if sky % 32 == 0 else 1
    finer = Mesh(mesh.devices.reshape(sky // (8 * near), near, 4, 2, tm), SKY + ("tm",))
    both = SKY + ("tm",)
    in_specs = (P(both, None, None), P(both, None), P(both, None, None), P(both, None))
    out_specs = (P(both, None, None), P(both, None, None))
    return jax.shard_map(local, mesh=finer, in_specs=in_specs, out_specs=out_specs, check_vma=False)
```

```python
import functools

import jax
import jax.numpy as jnp
from jax import lax
from jax.experimental import pallas as pl
from jax.experimental.pallas import tpu as pltpu
from jax.sharding import Mesh, PartitionSpec as P

F32 = jnp.float32
BF16 = jnp.bfloat16
BLOCKS, WIDTH, STARS, LANES = 2, 64, 512, 128
CHUNKS = STARS // LANES
NOISE = 3
LIST, IDENT, META = 3, 64, 4
SLOTS = 16
ROWS = STARS + CHUNKS * BLOCKS * META
NEAR = 18
OWN = 8
LONG, SHORT = 256, 64
AT_ONCE = {LONG: 4, SHORT: 8}
KEPT = {LONG: 40, SHORT: 48}
PADDED = STARS + LONG
NOTHING = STARS
FIRST = {LONG: 8, SHORT: 320}
COUNT = {LONG: 0, SHORT: 1}
LISTS = 512
VMEM = pl.BlockSpec(memory_space=pltpu.VMEM)
SMEM = pl.BlockSpec(memory_space=pltpu.SMEM)
FULL = 64 * 1024 * 1024
LIMIT = 32 * 1024 * 1024


def nt(left, right):
    return lax.dot_general(left, right, (((1,), (1,)), ((), ())), preferred_element_type=F32)


def nn(left, right):
    return lax.dot_general(left, right, (((1,), (0,)), ((), ())), preferred_element_type=F32)


def iota(shape, dim):
    return lax.broadcasted_iota(jnp.int32, shape, dim)


def column(row):
    return jnp.transpose(jnp.broadcast_to(row, (LANES, LANES)))


def lanes(chunk):
    return slice(chunk * LANES, (chunk + 1) * LANES)


def split_three(x):
    top = x.astype(BF16)
    rest = x - top.astype(F32)
    middle = rest.astype(BF16)
    return top, middle, (rest - middle.astype(F32)).astype(BF16)


def split_two(x):
    top = x.astype(BF16)
    return top, (x - top.astype(F32)).astype(BF16)


def one_hot(rank):
    same = iota((STARS, STARS), 0) == rank.astype(jnp.int32)
    return jnp.where(same, 1.0, 0.0).astype(BF16)


def fold(x):
    return x + pltpu.roll(x, WIDTH, axis=x.ndim - 1)


def left_half(rows):
    return iota((rows, LANES), 1) < WIDTH


def unsort(x, rank_ref, out_ref):
    turned = jnp.concatenate([jnp.transpose(x[lanes(jc), :]) for jc in range(CHUNKS)], axis=1)
    for b in range(BLOCKS):
        block = turned[b * WIDTH : (b + 1) * WIDTH]
        parts = nn(jnp.concatenate(split_three(block), axis=0), one_hot(rank_ref[b : b + 1, :]))
        out_ref[b] = (parts[:WIDTH] + parts[WIDTH : 2 * WIDTH]) + parts[2 * WIDTH :]


def ranks(times):
    counts = [jnp.zeros((1, LANES), F32) for _ in range(CHUNKS)]
    for jc in range(CHUNKS):
        other = column(times[:, lanes(jc)])
        for ic in range(CHUNKS):
            mine = times[:, lanes(ic)]
            if jc < ic:
                before = other <= mine
            elif jc > ic:
                before = other < mine
            else:
                earlier = iota((LANES, LANES), 0) < iota((LANES, LANES), 1)
                before = (other < mine) | ((other == mine) & earlier)
            counts[ic] += jnp.sum(jnp.where(before, 1.0, 0.0), axis=0, keepdims=True)
    return jnp.concatenate(counts, axis=1)


def meta_rows(b, jc):
    first = STARS + (jc * BLOCKS + b) * META
    return slice(first, first + META)


def sort_kernel(
    ident_ref, pos_hbm, noise_hbm, targets_hbm, list_hbm, packed_ref, rank_ref, noise_out, tall, small, *scratch
):
    pos_ref, noise_ref, targets_ref, list_ref, sems = scratch
    pairs = ((pos_hbm, pos_ref), (noise_hbm, noise_ref), (targets_hbm, targets_ref), (list_hbm, list_ref))
    copies = [pltpu.make_async_copy(a, b, sems.at[n]) for n, (a, b) in enumerate(pairs)]
    for copy in copies:
        copy.start()
    copies[0].wait()
    for b in range(BLOCKS):
        rank_ref[b : b + 1, :] = ranks(pos_ref[2, b : b + 1, :])
    for copy in copies[1:]:
        copy.wait()
    values = jnp.zeros((STARS, LANES), F32)
    for b in range(BLOCKS):
        where_to = one_hot(rank_ref[b : b + 1, :])
        tall[...] = jnp.zeros(tall.shape, F32)
        tall[b * WIDTH : (b + 1) * WIDTH, :] = targets_ref[b]
        parts = nt(where_to, jnp.concatenate(split_three(tall[...]), axis=0))
        values += (parts[:, lanes(0)] + parts[:, lanes(1)]) + parts[:, lanes(2)]
        small[...] = jnp.zeros(small.shape, F32)
        for c in range(3):
            small[c : c + 1, :] = pos_ref[c, b : b + 1, :]
        small[NOISE : NOISE + 1, :] = noise_ref[b : b + 1, :]
        parts = nt(jnp.concatenate(split_three(small[...]), axis=0), where_to)
        height = small.shape[0]
        meta = (parts[:height] + parts[height : 2 * height]) + parts[2 * height :]
        listed = list_ref[b : b + 1, :].astype(F32) + 1.0
        ident = jnp.full((1, LANES), (ident_ref[0] + b + 1).astype(F32))
        ident = jnp.where(iota((1, LANES), 1) < IDENT, 0.0, ident)
        for jc in range(CHUNKS):
            first = meta_rows(b, jc).start
            packed_ref[first : first + 3, :] = meta[0:3, lanes(jc)]
            noise_out[b * CHUNKS + jc : b * CHUNKS + jc + 1, :] = meta[NOISE : NOISE + 1, lanes(jc)]
            packed_ref[first + LIST : first + LIST + 1, :] = ident
            packed_ref[first + LIST : first + LIST + 1, 0 : listed.shape[1]] = listed
    packed_ref[0:STARS, :] = values


def build_table(places, blocks, own, own_times, chosen, table, turned):
    entries = blocks * CHUNKS
    turned[...] = jnp.zeros(turned.shape, F32)
    flipped = []
    for n, row in enumerate((2, LIST)):
        for at in range(entries):
            turned[n, at : at + 1, :] = places[at, row : row + 1, :]
        flipped.append(jnp.transpose(turned[n]))
    times, lists = flipped
    first, last = times[0:1, :], times[LANES - 1 : LANES, :]
    lists, ident = lists[0:SLOTS, :], lists[IDENT : IDENT + 1, :]
    entry = iota((1, LANES), 1)
    rows = []
    for o in range(BLOCKS):
        at = (own + o) * CHUNKS
        own_ident = turned[1, at : at + 1, IDENT : IDENT + 1]
        own_list = jnp.where(lists == 0.0, -5.0, lists)[:, at : at + 1]
        hit = jnp.where((lists == own_ident) | (own_list == ident), 1.0, 0.0)
        linked = (jnp.max(hit, axis=0, keepdims=True) > 0.0) | (ident == own_ident)
        linked = linked & chosen(entry) & (entry < entries)
        mine = own_times(o)
        skipped = jnp.sum(jnp.where(first - mine >= 1.0, 1.0, 0.0), axis=0, keepdims=True)
        beyond = jnp.sum(jnp.where(mine - last >= 1.0, 1.0, 0.0), axis=0, keepdims=True)
        start = skipped.astype(jnp.int32)
        end = STARS - beyond.astype(jnp.int32)
        start = start - (start & 7)
        count = jnp.where(linked & (end > start), end - start, 0)
        whole = (count + (LONG - SHORT - 1)) // LONG
        code = entry * 2048 + (o * PADDED + start)
        rows += [
            jnp.where(whole > 0, code, -1),
            jnp.where(count > whole * LONG, code + whole * LONG, -1),
            jnp.where(whole > 1, code + LONG, -1),
            jnp.where(whole > 1, 2, jnp.where(linked, 1, 0)),
        ]
    for n, row in enumerate(rows):
        table[n : n + 1, :] = row


def list_steps(table, tasks, blocks):
    def per_block(k, counts):
        for o in range(BLOCKS):
            flags = [table[4 * o + 3, CHUNKS * k + jc] for jc in range(CHUNKS)]

            def add(counts, o=o):
                counts = list(counts)
                codes = [[table[4 * o + n, CHUNKS * k + jc] for jc in range(CHUNKS)] for n in range(2)]
                for jc in range(CHUNKS):
                    for n, rows in enumerate((LONG, SHORT)):
                        tasks[FIRST[rows] + counts[n]] = codes[n][jc]
                        counts[n] += (codes[n][jc] >= 0).astype(jnp.int32)
                return tuple(counts)

            def more(counts, o=o):
                long, short = counts
                for jc in range(CHUNKS):
                    code = table[4 * o + 2, CHUNKS * k + jc]
                    tasks[FIRST[LONG] + long] = code
                    long += (code >= 0).astype(jnp.int32)
                return long, short

            counts = lax.cond(flags[0] > 0, add, lambda counts: counts, counts)
            most = jnp.maximum(jnp.maximum(flags[0], flags[1]), jnp.maximum(flags[2], flags[3]))
            counts = lax.cond(most > 1, more, lambda counts: counts, counts)
        return counts

    counts = lax.fori_loop(0, blocks, per_block, (jnp.int32(0), jnp.int32(0)))
    for rows, count in zip((LONG, SHORT), counts):
        tasks[COUNT[rows]] = count
        for n in range(AT_ONCE[rows]):
            tasks[FIRST[rows] + count + n] = NOTHING


def stage_weights(device, d, weights):
    left = left_half(LANES)
    for jc in range(CHUNKS):
        x = device[lanes(jc), :]
        top = x.astype(BF16).astype(F32)
        rest = pltpu.roll(x - top, WIDTH, axis=1)
        weights[2 * d * CHUNKS + jc] = jnp.where(left, top, rest).astype(BF16)
        weights[(2 * d + 1) * CHUNKS + jc] = jnp.where(left, rest, top).astype(BF16)


def eval_tile(at, row, rows, own_pos, places, tile):
    step = 64
    for piece in range(rows // step):
        squared = None
        for c in range(3):
            mine = own_pos[c, pl.ds(row + piece * step, step), :]
            offset = mine - places[at, c : c + 1, :]
            squared = offset * offset if squared is None else squared + offset * offset
        radius = squared * lax.rsqrt(jnp.maximum(squared, 1e-30))
        margin = jnp.maximum(1.0 - radius, 0.0)
        margin_sq = margin * margin
        values = (margin_sq * margin_sq) * (1.2 * radius + 0.3)
        top, rest = split_two(values)
        tile[piece * step : (piece + 1) * step, 0:LANES] = top
        tile[piece * step : (piece + 1) * step, LANES:] = rest


def decode(code):
    return code >> 11, pl.multiple_of(code & 2047, 8)


def add_product(at, row, rows, tile, weights, total):
    both = jnp.concatenate([weights[at], weights[at]], axis=0)
    total[pl.ds(row, rows), :] += nn(tile, both)


def run_steps(tasks, own_pos, places, weights, total, tiles, skip=None):
    for rows in (LONG, SHORT):
        width = AT_ONCE[rows]
        begin = skip[rows] // width if skip else 0

        def some(i, _):
            picked = [decode(tasks[FIRST[rows] + width * i + n]) for n in range(width)]
            for n in range(width + 1):
                if n < width:
                    at, row = picked[n]
                    eval_tile(at, row, rows, own_pos, places, tiles.at[n, 0:rows])
                if n > 0:
                    at, row = picked[n - 1]
                    add_product(at, row, rows, tiles[n - 1, 0:rows], weights, total)
            return 0

        lax.fori_loop(begin, (tasks[COUNT[rows]] + (width - 1)) // width, some, 0)


def keep_tiles(tasks, own_pos, places, kept):
    for rows in (LONG, SHORT):
        width = AT_ONCE[rows]

        def some(i, _):
            for n in range(width):
                at, row = decode(tasks[FIRST[rows] + width * i + n])
                eval_tile(at, row, rows, own_pos, places, kept[rows].at[width * i + n])
            return 0

        batches = (tasks[COUNT[rows]] + (width - 1)) // width
        lax.fori_loop(0, jnp.minimum(batches, KEPT[rows] // width), some, 0)


def run_kept(tasks, kept, weights, total):
    for rows in (LONG, SHORT):
        width = AT_ONCE[rows]

        def some(i, _):
            for n in range(width):
                at, row = decode(tasks[FIRST[rows] + width * i + n])
                add_product(at, row, rows, kept[rows][width * i + n], weights, total)
            return 0

        batches = (tasks[COUNT[rows]] + (width - 1)) // width
        lax.fori_loop(0, jnp.minimum(batches, KEPT[rows] // width), some, 0)


def own_rows(o):
    return slice(o * PADDED, o * PADDED + STARS)


def padding(o):
    return slice(o * PADDED + STARS, (o + 1) * PADDED)


def stage_own_sum(own_sum, total):
    for o in range(BLOCKS):
        total[own_rows(o), :] = own_sum[o * STARS : (o + 1) * STARS, :]
        total[padding(o), :] = jnp.zeros((PADDED - STARS, LANES), F32)


def image_of(total, own_pos, vector):
    left = left_half(STARS)
    noise = jnp.where(left, own_pos[NOISE, own_rows(0), :], own_pos[NOISE, own_rows(1), :])
    return noise * vector + jnp.where(left, fold(total[own_rows(0), :]), fold(total[own_rows(1), :]))


def stage_places(device, d, places):
    for b in range(BLOCKS):
        for jc in range(CHUNKS):
            places[(BLOCKS * d + b) * CHUNKS + jc, 0:META, :] = device[meta_rows(b, jc), :]


def own_kernel(packed, noise, own_pos, own_sum, places, own_tasks, weights, total, tiles, *scratch):
    turned, table, scalars, sem = scratch
    stage_places(packed, 0, places)
    for o in range(BLOCKS):
        for c in range(NOISE + 1):
            for ic in range(CHUNKS):
                first = o * PADDED + ic * LANES
                at = o * CHUNKS + ic
                row = noise[at : at + 1, :] if c == NOISE else places[at, c : c + 1, :]
                own_pos[c, first : first + LANES, :] = column(row)
            own_pos[c, padding(o), :] = jnp.zeros((PADDED - STARS, LANES), F32)
    build_table(places, BLOCKS, 0, lambda o: own_pos[2, own_rows(o), :], lambda e: e >= 0, table, turned)
    copy = pltpu.make_async_copy(table, scalars, sem)
    copy.start()
    stage_weights(packed, 0, weights)
    total[...] = jnp.zeros(total.shape, F32)
    copy.wait()
    list_steps(scalars, own_tasks, BLOCKS)
    run_steps(own_tasks, own_pos, places, weights, total, tiles)
    for o in range(BLOCKS):
        own_sum[o * STARS : (o + 1) * STARS, :] = total[own_rows(o), :]


def first_kernel(
    low, mid, high, own_pos, own_sum, image_ref, places, tasks, weights, total, tiles, *scratch
):
    turned, table, scalars, sem = scratch
    groups = (low, mid, high)
    devices = [groups[d // 3].at[d % 3] for d in range(9)]
    for d, device in enumerate(devices):
        stage_places(device, d, places)

    def others(entry):
        return (entry < OWN * CHUNKS) | (entry >= (OWN + BLOCKS) * CHUNKS)

    build_table(places, NEAR, OWN, lambda o: own_pos[2, own_rows(o), :], others, table, turned)
    copy = pltpu.make_async_copy(table, scalars, sem)
    copy.start()
    for d, device in enumerate(devices):
        if d != OWN // BLOCKS:
            stage_weights(device, d, weights)
    stage_own_sum(own_sum, total)
    copy.wait()
    list_steps(scalars, tasks, NEAR)
    run_steps(tasks, own_pos, places, weights, total, tiles)
    image_ref[...] = image_of(total, own_pos, mid[1, 0:STARS, :])


def between_kernel(
    own_tasks, tasks, once, own_pos, own_places, places, own_sum, kept_long, kept_short, weights, total, tiles
):
    stage_weights(once, 0, weights)
    total[...] = jnp.zeros(total.shape, F32)
    run_steps(own_tasks, own_pos, own_places, weights, total, tiles)
    for o in range(BLOCKS):
        own_sum[o * STARS : (o + 1) * STARS, :] = total[own_rows(o), :]
    keep_tiles(tasks, own_pos, places, {LONG: kept_long, SHORT: kept_short})


def second_kernel(
    tasks,
    low,
    mid,
    high,
    own_pos,
    own_sum,
    places,
    kept_long,
    kept_short,
    packed,
    rank,
    image_ref,
    moments_ref,
    weights,
    total,
    tiles,
    sums,
):
    groups = (low, mid, high)
    for d in range(9):
        if d != OWN // BLOCKS:
            stage_weights(groups[d // 3].at[d % 3], d, weights)
    stage_own_sum(own_sum, total)
    run_kept(tasks, {LONG: kept_long, SHORT: kept_short}, weights, total)
    run_steps(tasks, own_pos, places, weights, total, tiles, skip=KEPT)
    start, once = packed[0:STARS, :], mid[1]
    twice = image_of(total, own_pos, once)
    products = (start * start, start * once, once * once, start * twice, once * twice)
    sums[...] = jnp.zeros(sums.shape, F32)
    for n, product in enumerate(products):
        sums[n : n + 1, :] = jnp.sum(product, axis=0, keepdims=True)
    top, middle, rest = (part.astype(F32) for part in split_three(fold(sums[...])))
    moments_ref[...] = jnp.where(left_half(8), top, middle)
    for n in range(3):
        pair = jnp.where(left_half(1), rest[2 * n : 2 * n + 1, :], rest[2 * n + 1 : 2 * n + 2, :])
        moments_ref[5 + n : 6 + n, :] = pair
    unsort(twice, rank, image_ref)


def unsort_kernel(x_ref, rank_ref, out_ref):
    unsort(x_ref[...], rank_ref, out_ref)


def two_sum(a, b):
    s = a + b
    back = s - a
    return s, (a - (s - back)) + (b - back)


def halves(a):
    scaled = 4097.0 * a
    top = scaled - (scaled - a)
    return top, a - top


def two_product(a, b):
    p = a * b
    a1, a2 = halves(a)
    b1, b2 = halves(b)
    return p, ((a1 * b1 - p) + a1 * b2 + a2 * b1) + a2 * b2


def pair_add(a, b):
    s, e = two_sum(a[0], b[0])
    return two_sum(s, e + (a[1] + b[1]))


def pair_mul(a, b):
    p, e = two_product(a[0], b[0])
    return two_sum(p, e + (a[0] * b[1] + a[1] * b[0]))


def final_kernel(moments_ref, start_ref, once_ref, twice_ref, solution_ref, residual_ref):
    gathered = moments_ref[...]
    rolled = pltpu.roll(gathered, WIDTH, axis=1)
    left = iota((1, LANES), 1) < WIDTH
    moments = []
    for n in range(5):
        source = gathered if n % 2 == 0 else rolled
        last = source[5 + n // 2 : 6 + n // 2, :]
        s, e = two_sum(gathered[n : n + 1, :], rolled[n : n + 1, :])
        s, e = two_sum(s, e + last)
        moments.append((jnp.where(left, s, 1.0), jnp.where(left, e, 0.0)))
    norm, curve, square, cross, cube = moments
    alpha = norm[0] / curve[0]
    step = (alpha, jnp.zeros_like(alpha))
    minus = (-alpha, jnp.zeros_like(alpha))
    step_sq = pair_mul(step, step)
    by_curve = pair_mul(minus, curve)
    norm_next = pair_add(pair_add(norm, pair_add(by_curve, by_curve)), pair_mul(step_sq, square))
    beta = norm_next[0] / norm[0]
    gamma = two_sum(jnp.ones_like(beta), beta)
    curve_next = pair_add(
        pair_mul(pair_mul(gamma, gamma), curve),
        pair_add(
            pair_mul(pair_mul(gamma, minus), pair_add(cross, square)),
            pair_mul(step_sq, cube),
        ),
    )
    alpha_next = norm_next[0] / curve_next[0]
    alpha, beta, alpha_next = (column(row)[0:WIDTH] for row in (alpha, beta, alpha_next))
    for o in range(BLOCKS):
        for ic in range(CHUNKS):
            at = (o, slice(None), lanes(ic))
            start, once, twice = start_ref[at], once_ref[at], twice_ref[at]
            residual = start - alpha * once
            direction = residual + beta * start
            image = (once - alpha * twice) + beta * once
            solution_ref[at] = alpha * start + alpha_next * direction
            residual_ref[at] = residual - alpha_next * image


def shape(*dims, dtype=F32):
    return jax.ShapeDtypeStruct(dims, dtype)


def call(kernel, out_shape, scratch=(), in_specs=None, count=None, out_specs=None, limit=LIMIT, flops=0, nbytes=1 << 20):
    return pl.pallas_call(
        kernel,
        out_shape=out_shape,
        in_specs=in_specs if in_specs is not None else [VMEM] * count,
        out_specs=out_specs or jax.tree.map(lambda _: VMEM, out_shape),
        scratch_shapes=list(scratch),
        compiler_params=pltpu.CompilerParams(vmem_limit_bytes=limit),
        cost_estimate=pl.CostEstimate(flops=flops, bytes_accessed=nbytes, transcendentals=0),
    )


BLOCK = shape(BLOCKS, WIDTH, STARS)
OWN_POS = shape(NOISE + 1, BLOCKS * PADDED, LANES)
OWN_SUM = shape(BLOCKS * STARS, LANES)
TASKS = shape(LISTS, dtype=jnp.int32)


def pairs_scratch(blocks):
    return [
        pltpu.VMEM((blocks * CHUNKS, LANES, LANES), BF16),
        pltpu.VMEM((BLOCKS * PADDED, LANES), F32),
        pltpu.VMEM((max(AT_ONCE.values()), LONG, 2 * LANES), BF16),
    ]


TABLE_SCRATCH = [
    pltpu.VMEM((2, LANES, LANES), F32),
    pltpu.VMEM((8, LANES), jnp.int32),
    pltpu.SMEM((8, LANES), jnp.int32),
    pltpu.SemaphoreType.DMA,
]


def apply_own(packed, noise):
    return call(
        own_kernel,
        (OWN_POS, OWN_SUM, shape(BLOCKS * CHUNKS, 8, LANES), TASKS),
        scratch=pairs_scratch(BLOCKS) + TABLE_SCRATCH,
        count=2,
        out_specs=(VMEM, VMEM, VMEM, SMEM),
        flops=1 << 30,
    )(packed, noise)


def apply_first(low, mid, high, own_pos, own_sum):
    return call(
        first_kernel,
        (shape(STARS, LANES), shape(NEAR * CHUNKS, 8, LANES), TASKS),
        scratch=pairs_scratch(NEAR) + TABLE_SCRATCH,
        count=5,
        out_specs=(VMEM, VMEM, SMEM),
    )(low, mid, high, own_pos, own_sum)


def apply_between(own_tasks, tasks, once, own_pos, own_places, places):
    return call(
        between_kernel,
        (
            OWN_SUM,
            shape(KEPT[LONG], LONG, 2 * LANES, dtype=BF16),
            shape(KEPT[SHORT], SHORT, 2 * LANES, dtype=BF16),
        ),
        scratch=pairs_scratch(BLOCKS),
        in_specs=[SMEM, SMEM] + [VMEM] * 4,
        flops=1 << 30,
    )(own_tasks, tasks, once, own_pos, own_places, places)


def apply_second(tasks, low, mid, high, own_pos, own_sum, places, kept_long, kept_short, packed, rank):
    return call(
        second_kernel,
        (BLOCK, shape(8, LANES)),
        scratch=pairs_scratch(NEAR) + [pltpu.VMEM((8, LANES), F32)],
        in_specs=[SMEM] + [VMEM] * 10,
    )(tasks, low, mid, high, own_pos, own_sum, places, kept_long, kept_short, packed, rank)


def shift(x, axis, by):
    count = lax.axis_size(axis)
    return lax.ppermute(x, axis, [(i, i + by) for i in range(count) if 0 <= i + by < count])


SKY = ("far", "near", "x", "core")


def sky_shift(x, by):
    count = lax.axis_size(SKY)
    return lax.ppermute(x, SKY, [(i, i + by) for i in range(count) if 0 <= i + by < count])


def with_halo(x):
    before, after = shift(x, "tm", 1), shift(x, "tm", -1)
    mid = jnp.stack([before, x, after])
    return sky_shift(mid, 1), mid, sky_shift(mid, -1)


def local(star_pos, noise_var, targets, pair_list):
    ident = (lax.axis_index(SKY) * lax.axis_size("tm") + lax.axis_index("tm")) * BLOCKS
    hbm = pl.BlockSpec(memory_space=pltpu.HBM)
    stars = (BLOCKS, STARS)
    packed, rank, noise = call(
        sort_kernel,
        (shape(ROWS, LANES), shape(*stars), shape(BLOCKS * CHUNKS, LANES)),
        scratch=[
            pltpu.VMEM((BLOCKS * WIDTH, STARS), F32),
            pltpu.VMEM((16, STARS), F32),
            pltpu.VMEM((3,) + stars, F32),
            pltpu.VMEM(stars, F32),
            pltpu.VMEM((BLOCKS, WIDTH, STARS), F32),
            pltpu.VMEM(pair_list.shape, jnp.int32),
            pltpu.SemaphoreType.DMA((4,)),
        ],
        in_specs=[SMEM] + [hbm] * 4,
        limit=FULL - 512 * 1024,
    )(ident.reshape(1), jnp.swapaxes(star_pos, 0, 1), noise_var, targets, pair_list)
    low, mid, high = with_halo(packed)
    own_pos, own_sum, own_places, own_tasks = apply_own(packed, noise)
    once, places, tasks = apply_first(low, mid, high, own_pos, own_sum)
    low, mid, high = with_halo(once)
    own_sum, *kept = apply_between(own_tasks, tasks, once, own_pos, own_places, places)
    once_back = call(unsort_kernel, BLOCK, count=2, flops=1 << 28)(once, rank)
    twice_back, moments = apply_second(
        tasks, low, mid, high, own_pos, own_sum, places, *kept, packed, rank
    )
    for axis in ("core", "x", "tm", "near", "far"):
        moments = lax.psum(moments, axis)
    return call(final_kernel, (BLOCK, BLOCK), count=4)(moments, targets, once_back, twice_back)


def solution(mesh):
    sky, tm = mesh.devices.shape
    near = 4 if sky % 32 == 0 else 1
    finer = Mesh(mesh.devices.reshape(sky // (8 * near), near, 4, 2, tm), SKY + ("tm",))
    both = SKY + ("tm",)
    in_specs = (P(both, None, None), P(both, None), P(both, None, None), P(both, None))
    out_specs = (P(both, None, None), P(both, None, None))
    return jax.shard_map(local, mesh=finer, in_specs=in_specs, out_specs=out_specs, check_vma=False)
```

```python
import functools

import jax
import jax.numpy as jnp
from jax import lax
from jax.experimental import pallas as pl
from jax.experimental.pallas import tpu as pltpu
from jax.sharding import Mesh, PartitionSpec as P

F32 = jnp.float32
BF16 = jnp.bfloat16
BLOCKS, WIDTH, STARS, LANES = 2, 64, 512, 128
CHUNKS = STARS // LANES
NOISE = 3
LIST, IDENT, META = 3, 64, 4
SLOTS = 16
ROWS = STARS + CHUNKS * BLOCKS * META
NEAR = 18
OWN = 8
LONG, SHORT = 256, 64
AT_ONCE = {LONG: 4, SHORT: 8}
KEPT = {LONG: 40, SHORT: 48}
PADDED = STARS + LONG
NOTHING = STARS
COUNT = {LONG: 0, SHORT: 1}
FIRST = {LONG: 1, SHORT: 4}
LIST_ROWS = {LONG: 3, SHORT: 2}
VMEM = pl.BlockSpec(memory_space=pltpu.VMEM)
SMEM = pl.BlockSpec(memory_space=pltpu.SMEM)
FULL = 64 * 1024 * 1024
LIMIT = 32 * 1024 * 1024


def nt(left, right):
    return lax.dot_general(left, right, (((1,), (1,)), ((), ())), preferred_element_type=F32)


def nn(left, right):
    return lax.dot_general(left, right, (((1,), (0,)), ((), ())), preferred_element_type=F32)


def iota(shape, dim):
    return lax.broadcasted_iota(jnp.int32, shape, dim)


def column(row):
    return jnp.transpose(jnp.broadcast_to(row, (LANES, LANES)))


def lanes(chunk):
    return slice(chunk * LANES, (chunk + 1) * LANES)


def split_three(x):
    top = x.astype(BF16)
    rest = x - top.astype(F32)
    middle = rest.astype(BF16)
    return top, middle, (rest - middle.astype(F32)).astype(BF16)


def split_two(x):
    top = x.astype(BF16)
    return top, (x - top.astype(F32)).astype(BF16)


def one_hot(rank):
    same = iota((STARS, STARS), 0) == rank.astype(jnp.int32)
    return jnp.where(same, 1.0, 0.0).astype(BF16)


def fold(x):
    return x + pltpu.roll(x, WIDTH, axis=x.ndim - 1)


def left_half(rows):
    return iota((rows, LANES), 1) < WIDTH


def unsort(x, rank_ref, out_ref):
    turned = jnp.concatenate([jnp.transpose(x[lanes(jc), :]) for jc in range(CHUNKS)], axis=1)
    for b in range(BLOCKS):
        block = turned[b * WIDTH : (b + 1) * WIDTH]
        parts = nn(jnp.concatenate(split_three(block), axis=0), one_hot(rank_ref[b : b + 1, :]))
        out_ref[b] = (parts[:WIDTH] + parts[WIDTH : 2 * WIDTH]) + parts[2 * WIDTH :]


def ranks(times):
    counts = [jnp.zeros((1, LANES), F32) for _ in range(CHUNKS)]
    for jc in range(CHUNKS):
        other = column(times[:, lanes(jc)])
        for ic in range(CHUNKS):
            mine = times[:, lanes(ic)]
            if jc < ic:
                before = other <= mine
            elif jc > ic:
                before = other < mine
            else:
                earlier = iota((LANES, LANES), 0) < iota((LANES, LANES), 1)
                before = (other < mine) | ((other == mine) & earlier)
            counts[ic] += jnp.sum(jnp.where(before, 1.0, 0.0), axis=0, keepdims=True)
    return jnp.concatenate(counts, axis=1)


def meta_rows(b, jc):
    first = STARS + (jc * BLOCKS + b) * META
    return slice(first, first + META)


def sort_kernel(
    ident_ref, pos_hbm, noise_hbm, targets_hbm, list_hbm, packed_ref, rank_ref, noise_out, tall, small, *scratch
):
    pos_ref, noise_ref, targets_ref, list_ref, sems = scratch
    pairs = ((pos_hbm, pos_ref), (noise_hbm, noise_ref), (targets_hbm, targets_ref), (list_hbm, list_ref))
    copies = [pltpu.make_async_copy(a, b, sems.at[n]) for n, (a, b) in enumerate(pairs)]
    for copy in copies:
        copy.start()
    copies[0].wait()
    for b in range(BLOCKS):
        rank_ref[b : b + 1, :] = ranks(pos_ref[2, b : b + 1, :])
    for copy in copies[1:]:
        copy.wait()
    values = jnp.zeros((STARS, LANES), F32)
    for b in range(BLOCKS):
        where_to = one_hot(rank_ref[b : b + 1, :])
        tall[...] = jnp.zeros(tall.shape, F32)
        tall[b * WIDTH : (b + 1) * WIDTH, :] = targets_ref[b]
        parts = nt(where_to, jnp.concatenate(split_three(tall[...]), axis=0))
        values += (parts[:, lanes(0)] + parts[:, lanes(1)]) + parts[:, lanes(2)]
        small[...] = jnp.zeros(small.shape, F32)
        for c in range(3):
            small[c : c + 1, :] = pos_ref[c, b : b + 1, :]
        small[NOISE : NOISE + 1, :] = noise_ref[b : b + 1, :]
        parts = nt(jnp.concatenate(split_three(small[...]), axis=0), where_to)
        height = small.shape[0]
        meta = (parts[:height] + parts[height : 2 * height]) + parts[2 * height :]
        listed = list_ref[b : b + 1, :].astype(F32) + 1.0
        ident = jnp.full((1, LANES), (ident_ref[0] + b + 1).astype(F32))
        ident = jnp.where(iota((1, LANES), 1) < IDENT, 0.0, ident)
        for jc in range(CHUNKS):
            first = meta_rows(b, jc).start
            packed_ref[first : first + 3, :] = meta[0:3, lanes(jc)]
            noise_out[b * CHUNKS + jc : b * CHUNKS + jc + 1, :] = meta[NOISE : NOISE + 1, lanes(jc)]
            packed_ref[first + LIST : first + LIST + 1, :] = ident
            packed_ref[first + LIST : first + LIST + 1, 0 : listed.shape[1]] = listed
    packed_ref[0:STARS, :] = values


def build_lists(places, blocks, own, own_times, chosen, lists_out, turned):
    entries = blocks * CHUNKS
    turned[...] = jnp.zeros(turned.shape, F32)
    flipped = []
    for n, row in enumerate((2, LIST)):
        for at in range(entries):
            turned[n, at : at + 1, :] = places[at, row : row + 1, :]
        flipped.append(jnp.transpose(turned[n]))
    times, lists = flipped
    first, last = times[0:1, :], times[LANES - 1 : LANES, :]
    lists, ident = lists[0:SLOTS, :], lists[IDENT : IDENT + 1, :]
    entry = iota((1, LANES), 1)
    rows = {LONG: [], SHORT: []}
    for o in range(BLOCKS):
        at = (own + o) * CHUNKS
        own_ident = turned[1, at : at + 1, IDENT : IDENT + 1]
        own_list = jnp.where(lists == 0.0, -5.0, lists)[:, at : at + 1]
        hit = jnp.where((lists == own_ident) | (own_list == ident), 1.0, 0.0)
        linked = (jnp.max(hit, axis=0, keepdims=True) > 0.0) | (ident == own_ident)
        linked = linked & chosen(entry) & (entry < entries)
        mine = own_times(o)
        skipped = jnp.sum(jnp.where(first - mine >= 1.0, 1.0, 0.0), axis=0, keepdims=True)
        beyond = jnp.sum(jnp.where(mine - last >= 1.0, 1.0, 0.0), axis=0, keepdims=True)
        start = skipped.astype(jnp.int32)
        end = STARS - beyond.astype(jnp.int32)
        start = start - (start & 7)
        count = jnp.where(linked & (end > start), end - start, 0)
        whole = (count + (LONG - SHORT - 1)) // LONG
        code = entry * 2048 + (o * PADDED + start)
        rows[LONG].append(jnp.where(whole > 0, code, -1))
        rows[LONG].append(jnp.where(whole > 1, code + LONG, -1))
        rows[SHORT].append(jnp.where(count > whole * LONG, code + whole * LONG, -1))
    codes = [row.astype(F32) for row in rows[LONG] + rows[SHORT]]
    turned[0] = jnp.full((LANES, LANES), -1.0, F32)
    for n, row in enumerate(codes):
        turned[0, n : n + 1, :] = row
    flags = jnp.where(turned[0, 0:8, :] >= 0.0, 1.0, 0.0)
    earlier = jnp.where(iota((LANES, LANES), 0) < iota((LANES, LANES), 1), 1.0, 0.0)
    before = nn(flags.astype(BF16), earlier.astype(BF16))
    held = before[:, LANES - 1 :] + flags[:, LANES - 1 :]
    totals = {}
    n = 0
    for size in (LONG, SHORT):
        total = jnp.zeros((1, 1), F32)
        for _ in rows[size]:
            row = turned[0, n : n + 1, :]
            turned[0, 8 + n : 9 + n, :] = jnp.where(row >= 0.0, before[n : n + 1, :] + total, -1.0)
            total = total + held[n : n + 1, :]
            n += 1
        totals[size] = total
    columns = jnp.transpose(turned[0])
    lengths = jnp.where(entry == COUNT[LONG], totals[LONG], totals[SHORT])
    lists_out[0:1, :] = lengths.astype(jnp.int32)
    n = 0
    for size in (LONG, SHORT):
        picked = range(n, n + len(rows[size]))
        n += len(rows[size])
        for chunk in range(LIST_ROWS[size]):
            place = (iota((LANES, LANES), 1) + chunk * LANES).astype(F32)
            found = jnp.zeros((LANES, LANES), F32)
            for r in picked:
                found += jnp.where(columns[:, 8 + r : 9 + r] == place, columns[:, r : r + 1], 0.0)
            row = jnp.sum(found, axis=0, keepdims=True)
            row = jnp.where(place[0:1, :] < totals[size], row, float(NOTHING))
            lists_out[FIRST[size] + chunk : FIRST[size] + chunk + 1, :] = row.astype(jnp.int32)


def stage_weights(device, d, weights):
    left = left_half(LANES)
    for jc in range(CHUNKS):
        x = device[lanes(jc), :]
        top = x.astype(BF16).astype(F32)
        rest = pltpu.roll(x - top, WIDTH, axis=1)
        weights[2 * d * CHUNKS + jc] = jnp.where(left, top, rest).astype(BF16)
        weights[(2 * d + 1) * CHUNKS + jc] = jnp.where(left, rest, top).astype(BF16)


def eval_tile(at, row, rows, own_pos, places, tile):
    step = 64
    for piece in range(rows // step):
        squared = None
        for c in range(3):
            mine = own_pos[c, pl.ds(row + piece * step, step), :]
            offset = mine - places[at, c : c + 1, :]
            squared = offset * offset if squared is None else squared + offset * offset
        radius = squared * lax.rsqrt(jnp.maximum(squared, 1e-30))
        margin = jnp.maximum(1.0 - radius, 0.0)
        margin_sq = margin * margin
        values = (margin_sq * margin_sq) * (1.2 * radius + 0.3)
        top, rest = split_two(values)
        tile[piece * step : (piece + 1) * step, 0:LANES] = top
        tile[piece * step : (piece + 1) * step, LANES:] = rest


def step_at(tasks, rows, n):
    code = tasks[FIRST[rows] + (n >> 7), n & 127]
    return code >> 11, pl.multiple_of(code & 2047, 8)


def length(tasks, rows):
    return tasks[0, COUNT[rows]]


def add_product(at, row, rows, tile, weights, total):
    both = jnp.concatenate([weights[at], weights[at]], axis=0)
    total[pl.ds(row, rows), :] += nn(tile, both)


def run_steps(tasks, own_pos, places, weights, total, tiles, skip=None):
    for rows in (LONG, SHORT):
        width = AT_ONCE[rows]
        begin = skip[rows] // width if skip else 0

        def some(i, _):
            picked = [step_at(tasks, rows, width * i + n) for n in range(width)]
            for n in range(width + 1):
                if n < width:
                    at, row = picked[n]
                    eval_tile(at, row, rows, own_pos, places, tiles.at[n, 0:rows])
                if n > 0:
                    at, row = picked[n - 1]
                    add_product(at, row, rows, tiles[n - 1, 0:rows], weights, total)
            return 0

        lax.fori_loop(begin, (length(tasks, rows) + (width - 1)) // width, some, 0)


def keep_tiles(tasks, own_pos, places, kept):
    for rows in (LONG, SHORT):
        width = AT_ONCE[rows]

        def some(i, _):
            for n in range(width):
                at, row = step_at(tasks, rows, width * i + n)
                eval_tile(at, row, rows, own_pos, places, kept[rows].at[width * i + n])
            return 0

        batches = (length(tasks, rows) + (width - 1)) // width
        lax.fori_loop(0, jnp.minimum(batches, KEPT[rows] // width), some, 0)


def run_kept(tasks, kept, weights, total):
    for rows in (LONG, SHORT):
        width = AT_ONCE[rows]

        def some(i, _):
            for n in range(width):
                at, row = step_at(tasks, rows, width * i + n)
                add_product(at, row, rows, kept[rows][width * i + n], weights, total)
            return 0

        batches = (length(tasks, rows) + (width - 1)) // width
        lax.fori_loop(0, jnp.minimum(batches, KEPT[rows] // width), some, 0)


def own_rows(o):
    return slice(o * PADDED, o * PADDED + STARS)


def padding(o):
    return slice(o * PADDED + STARS, (o + 1) * PADDED)


def stage_own_sum(own_sum, total):
    for o in range(BLOCKS):
        total[own_rows(o), :] = own_sum[o * STARS : (o + 1) * STARS, :]
        total[padding(o), :] = jnp.zeros((PADDED - STARS, LANES), F32)


def image_of(total, own_pos, vector):
    left = left_half(STARS)
    noise = jnp.where(left, own_pos[NOISE, own_rows(0), :], own_pos[NOISE, own_rows(1), :])
    return noise * vector + jnp.where(left, fold(total[own_rows(0), :]), fold(total[own_rows(1), :]))


def stage_places(device, d, places):
    for b in range(BLOCKS):
        for jc in range(CHUNKS):
            places[(BLOCKS * d + b) * CHUNKS + jc, 0:META, :] = device[meta_rows(b, jc), :]


def own_kernel(packed, noise, own_pos, own_sum, places, own_tasks, weights, total, tiles, *scratch):
    turned, lists, sem = scratch
    stage_places(packed, 0, places)
    for o in range(BLOCKS):
        for c in range(NOISE + 1):
            for ic in range(CHUNKS):
                first = o * PADDED + ic * LANES
                at = o * CHUNKS + ic
                row = noise[at : at + 1, :] if c == NOISE else places[at, c : c + 1, :]
                own_pos[c, first : first + LANES, :] = column(row)
            own_pos[c, padding(o), :] = jnp.zeros((PADDED - STARS, LANES), F32)
    build_lists(places, BLOCKS, 0, lambda o: own_pos[2, own_rows(o), :], lambda e: e >= 0, lists, turned)
    copy = pltpu.make_async_copy(lists, own_tasks, sem)
    copy.start()
    stage_weights(packed, 0, weights)
    total[...] = jnp.zeros(total.shape, F32)
    copy.wait()
    run_steps(own_tasks, own_pos, places, weights, total, tiles)
    for o in range(BLOCKS):
        own_sum[o * STARS : (o + 1) * STARS, :] = total[own_rows(o), :]


def first_kernel(
    low, mid, high, own_pos, own_sum, image_ref, places, tasks, weights, total, tiles, *scratch
):
    turned, lists, sem = scratch
    groups = (low, mid, high)
    devices = [groups[d // 3].at[d % 3] for d in range(9)]
    for d, device in enumerate(devices):
        stage_places(device, d, places)

    def others(entry):
        return (entry < OWN * CHUNKS) | (entry >= (OWN + BLOCKS) * CHUNKS)

    build_lists(places, NEAR, OWN, lambda o: own_pos[2, own_rows(o), :], others, lists, turned)
    copy = pltpu.make_async_copy(lists, tasks, sem)
    copy.start()
    for d, device in enumerate(devices):
        if d != OWN // BLOCKS:
            stage_weights(device, d, weights)
    stage_own_sum(own_sum, total)
    copy.wait()
    run_steps(tasks, own_pos, places, weights, total, tiles)
    image_ref[...] = image_of(total, own_pos, mid[1, 0:STARS, :])


def between_kernel(
    own_tasks, tasks, once, own_pos, own_places, places, own_sum, kept_long, kept_short, weights, total, tiles
):
    stage_weights(once, 0, weights)
    total[...] = jnp.zeros(total.shape, F32)
    run_steps(own_tasks, own_pos, own_places, weights, total, tiles)
    for o in range(BLOCKS):
        own_sum[o * STARS : (o + 1) * STARS, :] = total[own_rows(o), :]
    keep_tiles(tasks, own_pos, places, {LONG: kept_long, SHORT: kept_short})


def second_kernel(
    tasks,
    low,
    mid,
    high,
    own_pos,
    own_sum,
    places,
    kept_long,
    kept_short,
    packed,
    rank,
    image_ref,
    moments_ref,
    weights,
    total,
    tiles,
    sums,
):
    groups = (low, mid, high)
    for d in range(9):
        if d != OWN // BLOCKS:
            stage_weights(groups[d // 3].at[d % 3], d, weights)
    stage_own_sum(own_sum, total)
    run_kept(tasks, {LONG: kept_long, SHORT: kept_short}, weights, total)
    run_steps(tasks, own_pos, places, weights, total, tiles, skip=KEPT)
    start, once = packed[0:STARS, :], mid[1]
    twice = image_of(total, own_pos, once)
    products = (start * start, start * once, once * once, start * twice, once * twice)
    sums[...] = jnp.zeros(sums.shape, F32)
    for n, product in enumerate(products):
        sums[n : n + 1, :] = jnp.sum(product, axis=0, keepdims=True)
    top, middle, rest = (part.astype(F32) for part in split_three(fold(sums[...])))
    moments_ref[...] = jnp.where(left_half(8), top, middle)
    for n in range(3):
        pair = jnp.where(left_half(1), rest[2 * n : 2 * n + 1, :], rest[2 * n + 1 : 2 * n + 2, :])
        moments_ref[5 + n : 6 + n, :] = pair
    unsort(twice, rank, image_ref)


def unsort_kernel(x_ref, rank_ref, out_ref):
    unsort(x_ref[...], rank_ref, out_ref)


def two_sum(a, b):
    s = a + b
    back = s - a
    return s, (a - (s - back)) + (b - back)


def halves(a):
    scaled = 4097.0 * a
    top = scaled - (scaled - a)
    return top, a - top


def two_product(a, b):
    p = a * b
    a1, a2 = halves(a)
    b1, b2 = halves(b)
    return p, ((a1 * b1 - p) + a1 * b2 + a2 * b1) + a2 * b2


def pair_add(a, b):
    s, e = two_sum(a[0], b[0])
    return two_sum(s, e + (a[1] + b[1]))


def pair_mul(a, b):
    p, e = two_product(a[0], b[0])
    return two_sum(p, e + (a[0] * b[1] + a[1] * b[0]))


def final_kernel(moments_ref, start_ref, once_ref, twice_ref, solution_ref, residual_ref):
    gathered = moments_ref[...]
    rolled = pltpu.roll(gathered, WIDTH, axis=1)
    left = iota((1, LANES), 1) < WIDTH
    moments = []
    for n in range(5):
        source = gathered if n % 2 == 0 else rolled
        last = source[5 + n // 2 : 6 + n // 2, :]
        s, e = two_sum(gathered[n : n + 1, :], rolled[n : n + 1, :])
        s, e = two_sum(s, e + last)
        moments.append((jnp.where(left, s, 1.0), jnp.where(left, e, 0.0)))
    norm, curve, square, cross, cube = moments
    alpha = norm[0] / curve[0]
    step = (alpha, jnp.zeros_like(alpha))
    minus = (-alpha, jnp.zeros_like(alpha))
    step_sq = pair_mul(step, step)
    by_curve = pair_mul(minus, curve)
    norm_next = pair_add(pair_add(norm, pair_add(by_curve, by_curve)), pair_mul(step_sq, square))
    beta = norm_next[0] / norm[0]
    gamma = two_sum(jnp.ones_like(beta), beta)
    curve_next = pair_add(
        pair_mul(pair_mul(gamma, gamma), curve),
        pair_add(
            pair_mul(pair_mul(gamma, minus), pair_add(cross, square)),
            pair_mul(step_sq, cube),
        ),
    )
    alpha_next = norm_next[0] / curve_next[0]
    alpha, beta, alpha_next = (column(row)[0:WIDTH] for row in (alpha, beta, alpha_next))
    for o in range(BLOCKS):
        for ic in range(CHUNKS):
            at = (o, slice(None), lanes(ic))
            start, once, twice = start_ref[at], once_ref[at], twice_ref[at]
            residual = start - alpha * once
            direction = residual + beta * start
            image = (once - alpha * twice) + beta * once
            solution_ref[at] = alpha * start + alpha_next * direction
            residual_ref[at] = residual - alpha_next * image


def shape(*dims, dtype=F32):
    return jax.ShapeDtypeStruct(dims, dtype)


def call(kernel, out_shape, scratch=(), in_specs=None, count=None, out_specs=None, limit=LIMIT, flops=0, nbytes=1 << 20):
    return pl.pallas_call(
        kernel,
        out_shape=out_shape,
        in_specs=in_specs if in_specs is not None else [VMEM] * count,
        out_specs=out_specs or jax.tree.map(lambda _: VMEM, out_shape),
        scratch_shapes=list(scratch),
        compiler_params=pltpu.CompilerParams(vmem_limit_bytes=limit),
        cost_estimate=pl.CostEstimate(flops=flops, bytes_accessed=nbytes, transcendentals=0),
    )


BLOCK = shape(BLOCKS, WIDTH, STARS)
OWN_POS = shape(NOISE + 1, BLOCKS * PADDED, LANES)
OWN_SUM = shape(BLOCKS * STARS, LANES)
TASKS = shape(8, LANES, dtype=jnp.int32)


def pairs_scratch(blocks):
    return [
        pltpu.VMEM((blocks * CHUNKS, LANES, LANES), BF16),
        pltpu.VMEM((BLOCKS * PADDED, LANES), F32),
        pltpu.VMEM((max(AT_ONCE.values()), LONG, 2 * LANES), BF16),
    ]


LIST_SCRATCH = [
    pltpu.VMEM((2, LANES, LANES), F32),
    pltpu.VMEM((8, LANES), jnp.int32),
    pltpu.SemaphoreType.DMA,
]


def apply_own(packed, noise):
    return call(
        own_kernel,
        (OWN_POS, OWN_SUM, shape(BLOCKS * CHUNKS, 8, LANES), TASKS),
        scratch=pairs_scratch(BLOCKS) + LIST_SCRATCH,
        count=2,
        out_specs=(VMEM, VMEM, VMEM, SMEM),
        flops=1 << 30,
    )(packed, noise)


def apply_first(low, mid, high, own_pos, own_sum):
    return call(
        first_kernel,
        (shape(STARS, LANES), shape(NEAR * CHUNKS, 8, LANES), TASKS),
        scratch=pairs_scratch(NEAR) + LIST_SCRATCH,
        count=5,
        out_specs=(VMEM, VMEM, SMEM),
    )(low, mid, high, own_pos, own_sum)


def apply_between(own_tasks, tasks, once, own_pos, own_places, places):
    return call(
        between_kernel,
        (
            OWN_SUM,
            shape(KEPT[LONG], LONG, 2 * LANES, dtype=BF16),
            shape(KEPT[SHORT], SHORT, 2 * LANES, dtype=BF16),
        ),
        scratch=pairs_scratch(BLOCKS),
        in_specs=[SMEM, SMEM] + [VMEM] * 4,
        flops=1 << 30,
    )(own_tasks, tasks, once, own_pos, own_places, places)


def apply_second(tasks, low, mid, high, own_pos, own_sum, places, kept_long, kept_short, packed, rank):
    return call(
        second_kernel,
        (BLOCK, shape(8, LANES)),
        scratch=pairs_scratch(NEAR) + [pltpu.VMEM((8, LANES), F32)],
        in_specs=[SMEM] + [VMEM] * 10,
    )(tasks, low, mid, high, own_pos, own_sum, places, kept_long, kept_short, packed, rank)


def shift(x, axis, by):
    count = lax.axis_size(axis)
    return lax.ppermute(x, axis, [(i, i + by) for i in range(count) if 0 <= i + by < count])


SKY = ("far", "near", "x", "core")


def sky_shift(x, by):
    count = lax.axis_size(SKY)
    return lax.ppermute(x, SKY, [(i, i + by) for i in range(count) if 0 <= i + by < count])


def with_halo(x):
    before, after = shift(x, "tm", 1), shift(x, "tm", -1)
    mid = lax.optimization_barrier(jnp.zeros((3,) + x.shape, F32).at[1].set(x))
    mid = mid.at[0].set(before).at[2].set(after)
    return sky_shift(mid, 1), mid, sky_shift(mid, -1)


def local(star_pos, noise_var, targets, pair_list):
    ident = (lax.axis_index(SKY) * lax.axis_size("tm") + lax.axis_index("tm")) * BLOCKS
    hbm = pl.BlockSpec(memory_space=pltpu.HBM)
    stars = (BLOCKS, STARS)
    packed, rank, noise = call(
        sort_kernel,
        (shape(ROWS, LANES), shape(*stars), shape(BLOCKS * CHUNKS, LANES)),
        scratch=[
            pltpu.VMEM((BLOCKS * WIDTH, STARS), F32),
            pltpu.VMEM((16, STARS), F32),
            pltpu.VMEM((3,) + stars, F32),
            pltpu.VMEM(stars, F32),
            pltpu.VMEM((BLOCKS, WIDTH, STARS), F32),
            pltpu.VMEM(pair_list.shape, jnp.int32),
            pltpu.SemaphoreType.DMA((4,)),
        ],
        in_specs=[SMEM] + [hbm] * 4,
        limit=FULL - 512 * 1024,
    )(ident.reshape(1), jnp.swapaxes(star_pos, 0, 1), noise_var, targets, pair_list)
    low, mid, high = with_halo(packed)
    own_pos, own_sum, own_places, own_tasks = apply_own(packed, noise)
    once, places, tasks = apply_first(low, mid, high, own_pos, own_sum)
    low, mid, high = with_halo(once)
    own_sum, *kept = apply_between(own_tasks, tasks, once, own_pos, own_places, places)
    once_back = call(unsort_kernel, BLOCK, count=2, flops=1 << 28)(once, rank)
    twice_back, moments = apply_second(
        tasks, low, mid, high, own_pos, own_sum, places, *kept, packed, rank
    )
    for axis in ("core", "x", "tm", "near", "far"):
        moments = lax.psum(moments, axis)
    return call(final_kernel, (BLOCK, BLOCK), count=4)(moments, targets, once_back, twice_back)


def solution(mesh):
    sky, tm = mesh.devices.shape
    near = 4 if sky % 32 == 0 else 1
    finer = Mesh(mesh.devices.reshape(sky // (8 * near), near, 4, 2, tm), SKY + ("tm",))
    both = SKY + ("tm",)
    in_specs = (P(both, None, None), P(both, None), P(both, None, None), P(both, None))
    out_specs = (P(both, None, None), P(both, None, None))
    return jax.shard_map(local, mesh=finer, in_specs=in_specs, out_specs=out_specs, check_vma=False)
```

```python
import functools

import jax
import jax.numpy as jnp
from jax import lax
from jax.experimental import pallas as pl
from jax.experimental.pallas import tpu as pltpu
from jax.sharding import Mesh, PartitionSpec as P

F32 = jnp.float32
BF16 = jnp.bfloat16
BLOCKS, WIDTH, STARS, LANES = 2, 64, 512, 128
CHUNKS = STARS // LANES
NOISE = 3
LIST, IDENT, META = 3, 64, 4
SLOTS = 16
ROWS = STARS + CHUNKS * BLOCKS * META
NEAR = 18
OWN = 8
LONG, SHORT = 256, 64
AT_ONCE = {LONG: 4, SHORT: 8}
AT_END = {LONG: 1, SHORT: 4}
FEW = {LONG: 2, SHORT: 4}
KEPT = {LONG: 40, SHORT: 48}
PADDED = STARS + LONG
NOTHING = STARS
COUNT = {LONG: 0, SHORT: 1}
FIRST = {LONG: 1, SHORT: 4}
LIST_ROWS = {LONG: 3, SHORT: 2}
VMEM = pl.BlockSpec(memory_space=pltpu.VMEM)
SMEM = pl.BlockSpec(memory_space=pltpu.SMEM)
FULL = 64 * 1024 * 1024
LIMIT = 32 * 1024 * 1024


def nt(left, right):
    return lax.dot_general(left, right, (((1,), (1,)), ((), ())), preferred_element_type=F32)


def nn(left, right):
    return lax.dot_general(left, right, (((1,), (0,)), ((), ())), preferred_element_type=F32)


def iota(shape, dim):
    return lax.broadcasted_iota(jnp.int32, shape, dim)


def column(row):
    return jnp.transpose(jnp.broadcast_to(row, (LANES, LANES)))


def lanes(chunk):
    return slice(chunk * LANES, (chunk + 1) * LANES)


def split_three(x):
    top = x.astype(BF16)
    rest = x - top.astype(F32)
    middle = rest.astype(BF16)
    return top, middle, (rest - middle.astype(F32)).astype(BF16)


def split_two(x):
    top = x.astype(BF16)
    return top, (x - top.astype(F32)).astype(BF16)


def one_hot(rank):
    same = iota((STARS, STARS), 0) == rank.astype(jnp.int32)
    return jnp.where(same, 1.0, 0.0).astype(BF16)


def fold(x):
    return x + pltpu.roll(x, WIDTH, axis=x.ndim - 1)


def left_half(rows):
    return iota((rows, LANES), 1) < WIDTH


def unsort(x, rank_ref, out_ref):
    turned = jnp.concatenate([jnp.transpose(x[lanes(jc), :]) for jc in range(CHUNKS)], axis=1)
    for b in range(BLOCKS):
        block = turned[b * WIDTH : (b + 1) * WIDTH]
        parts = nn(jnp.concatenate(split_three(block), axis=0), one_hot(rank_ref[b : b + 1, :]))
        out_ref[b] = (parts[:WIDTH] + parts[WIDTH : 2 * WIDTH]) + parts[2 * WIDTH :]


def ranks(times):
    counts = [jnp.zeros((1, LANES), F32) for _ in range(CHUNKS)]
    for jc in range(CHUNKS):
        other = column(times[:, lanes(jc)])
        for ic in range(CHUNKS):
            mine = times[:, lanes(ic)]
            if jc < ic:
                before = other <= mine
            elif jc > ic:
                before = other < mine
            else:
                earlier = iota((LANES, LANES), 0) < iota((LANES, LANES), 1)
                before = (other < mine) | ((other == mine) & earlier)
            counts[ic] += jnp.sum(jnp.where(before, 1.0, 0.0), axis=0, keepdims=True)
    return jnp.concatenate(counts, axis=1)


def meta_rows(b, jc):
    first = STARS + (jc * BLOCKS + b) * META
    return slice(first, first + META)


def sort_kernel(
    ident_ref, pos_hbm, noise_hbm, targets_hbm, list_hbm, packed_ref, rank_ref, noise_out, tall, small, *scratch
):
    pos_ref, noise_ref, targets_ref, list_ref, sems = scratch
    pairs = ((pos_hbm, pos_ref), (noise_hbm, noise_ref), (targets_hbm, targets_ref), (list_hbm, list_ref))
    copies = [pltpu.make_async_copy(a, b, sems.at[n]) for n, (a, b) in enumerate(pairs)]
    for copy in copies:
        copy.start()
    copies[0].wait()
    for b in range(BLOCKS):
        rank_ref[b : b + 1, :] = ranks(pos_ref[2, b : b + 1, :])
    for copy in copies[1:]:
        copy.wait()
    values = jnp.zeros((STARS, LANES), F32)
    for b in range(BLOCKS):
        where_to = one_hot(rank_ref[b : b + 1, :])
        tall[...] = jnp.zeros(tall.shape, F32)
        tall[b * WIDTH : (b + 1) * WIDTH, :] = targets_ref[b]
        parts = nt(where_to, jnp.concatenate(split_three(tall[...]), axis=0))
        values += (parts[:, lanes(0)] + parts[:, lanes(1)]) + parts[:, lanes(2)]
        small[...] = jnp.zeros(small.shape, F32)
        for c in range(3):
            small[c : c + 1, :] = pos_ref[c, b : b + 1, :]
        small[NOISE : NOISE + 1, :] = noise_ref[b : b + 1, :]
        parts = nt(jnp.concatenate(split_three(small[...]), axis=0), where_to)
        height = small.shape[0]
        meta = (parts[:height] + parts[height : 2 * height]) + parts[2 * height :]
        listed = list_ref[b : b + 1, :].astype(F32) + 1.0
        ident = jnp.full((1, LANES), (ident_ref[0] + b + 1).astype(F32))
        ident = jnp.where(iota((1, LANES), 1) < IDENT, 0.0, ident)
        for jc in range(CHUNKS):
            first = meta_rows(b, jc).start
            packed_ref[first : first + 3, :] = meta[0:3, lanes(jc)]
            noise_out[b * CHUNKS + jc : b * CHUNKS + jc + 1, :] = meta[NOISE : NOISE + 1, lanes(jc)]
            packed_ref[first + LIST : first + LIST + 1, :] = ident
            packed_ref[first + LIST : first + LIST + 1, 0 : listed.shape[1]] = listed
    packed_ref[0:STARS, :] = values


def build_lists(places, blocks, own, own_times, chosen, lists_out, turned):
    entries = blocks * CHUNKS
    turned[...] = jnp.zeros(turned.shape, F32)
    flipped = []
    for n, row in enumerate((2, LIST)):
        for at in range(entries):
            turned[n, at : at + 1, :] = places[at, row : row + 1, :]
        flipped.append(jnp.transpose(turned[n]))
    times, lists = flipped
    first, last = times[0:1, :], times[LANES - 1 : LANES, :]
    lists, ident = lists[0:SLOTS, :], lists[IDENT : IDENT + 1, :]
    entry = iota((1, LANES), 1)
    rows = {LONG: [], SHORT: []}
    for o in range(BLOCKS):
        at = (own + o) * CHUNKS
        own_ident = turned[1, at : at + 1, IDENT : IDENT + 1]
        own_list = jnp.where(lists == 0.0, -5.0, lists)[:, at : at + 1]
        hit = jnp.where((lists == own_ident) | (own_list == ident), 1.0, 0.0)
        linked = (jnp.max(hit, axis=0, keepdims=True) > 0.0) | (ident == own_ident)
        linked = linked & chosen(entry) & (entry < entries)
        mine = own_times(o)
        skipped = jnp.sum(jnp.where(first - mine >= 1.0, 1.0, 0.0), axis=0, keepdims=True)
        beyond = jnp.sum(jnp.where(mine - last >= 1.0, 1.0, 0.0), axis=0, keepdims=True)
        start = skipped.astype(jnp.int32)
        end = STARS - beyond.astype(jnp.int32)
        start = start - (start & 7)
        count = jnp.where(linked & (end > start), end - start, 0)
        whole = (count + (LONG - SHORT - 1)) // LONG
        code = entry * 2048 + (o * PADDED + start)
        rows[LONG].append(jnp.where(whole > 0, code, -1))
        rows[LONG].append(jnp.where(whole > 1, code + LONG, -1))
        rows[SHORT].append(jnp.where(count > whole * LONG, code + whole * LONG, -1))
    codes = [row.astype(F32) for row in rows[LONG] + rows[SHORT]]
    turned[0] = jnp.full((LANES, LANES), -1.0, F32)
    for n, row in enumerate(codes):
        turned[0, n : n + 1, :] = row
    flags = jnp.where(turned[0, 0:8, :] >= 0.0, 1.0, 0.0)
    earlier = jnp.where(iota((LANES, LANES), 0) < iota((LANES, LANES), 1), 1.0, 0.0)
    before = nn(flags.astype(BF16), earlier.astype(BF16))
    held = before[:, LANES - 1 :] + flags[:, LANES - 1 :]
    totals = {}
    n = 0
    for size in (LONG, SHORT):
        total = jnp.zeros((1, 1), F32)
        for _ in rows[size]:
            row = turned[0, n : n + 1, :]
            turned[0, 8 + n : 9 + n, :] = jnp.where(row >= 0.0, before[n : n + 1, :] + total, -1.0)
            total = total + held[n : n + 1, :]
            n += 1
        totals[size] = total
    columns = jnp.transpose(turned[0])
    lengths = jnp.where(entry == COUNT[LONG], totals[LONG], totals[SHORT])
    lists_out[0:1, :] = lengths.astype(jnp.int32)
    n = 0
    for size in (LONG, SHORT):
        picked = range(n, n + len(rows[size]))
        n += len(rows[size])
        for chunk in range(LIST_ROWS[size]):
            place = (iota((LANES, LANES), 1) + chunk * LANES).astype(F32)
            found = jnp.zeros((LANES, LANES), F32)
            for r in picked:
                found += jnp.where(columns[:, 8 + r : 9 + r] == place, columns[:, r : r + 1], 0.0)
            row = jnp.sum(found, axis=0, keepdims=True)
            row = jnp.where(place[0:1, :] < totals[size], row, float(NOTHING))
            lists_out[FIRST[size] + chunk : FIRST[size] + chunk + 1, :] = row.astype(jnp.int32)


def stage_weights(device, d, weights):
    left = left_half(LANES)
    for jc in range(CHUNKS):
        x = device[lanes(jc), :]
        top = x.astype(BF16).astype(F32)
        rest = pltpu.roll(x - top, WIDTH, axis=1)
        weights[2 * d * CHUNKS + jc] = jnp.where(left, top, rest).astype(BF16)
        weights[(2 * d + 1) * CHUNKS + jc] = jnp.where(left, rest, top).astype(BF16)


def eval_tile(at, row, rows, own_pos, places, tile):
    step = 64
    for piece in range(rows // step):
        squared = None
        for c in range(3):
            mine = own_pos[c, pl.ds(row + piece * step, step), :]
            offset = mine - places[at, c : c + 1, :]
            squared = offset * offset if squared is None else squared + offset * offset
        radius = squared * lax.rsqrt(jnp.maximum(squared, 1e-30))
        margin = jnp.maximum(1.0 - radius, 0.0)
        margin_sq = margin * margin
        values = (margin_sq * margin_sq) * (1.2 * radius + 0.3)
        top, rest = split_two(values)
        tile[piece * step : (piece + 1) * step, 0:LANES] = top
        tile[piece * step : (piece + 1) * step, LANES:] = rest


def step_at(tasks, rows, n):
    code = tasks[FIRST[rows] + (n >> 7), n & 127]
    return code >> 11, pl.multiple_of(code & 2047, 8)


def length(tasks, rows):
    return tasks[0, COUNT[rows]]


def add_product(at, row, rows, tile, weights, total):
    both = jnp.concatenate([weights[at], weights[at]], axis=0)
    total[pl.ds(row, rows), :] += nn(tile, both)


def in_batches(tasks, rows, first, last, some):
    width, narrow = AT_ONCE[rows], AT_END[rows]
    shift_wide, shift_narrow = width.bit_length() - 1, narrow.bit_length() - 1

    def wide(i, _):
        some(first + width * i, width)
        return 0

    whole = (jnp.maximum(last - first, 0) + (width - 1 - FEW[rows])) >> shift_wide
    lax.fori_loop(0, whole, wide, 0)
    rest = first + width * whole

    def few(i, _):
        some(rest + narrow * i, narrow)
        return 0

    lax.fori_loop(0, (jnp.maximum(last - rest, 0) + (narrow - 1)) >> shift_narrow, few, 0)


def run_steps(tasks, own_pos, places, weights, total, tiles, skip=None):
    for rows in (LONG, SHORT):

        def some(first, width, rows=rows):
            picked = [step_at(tasks, rows, first + n) for n in range(width)]
            for n in range(width + 1):
                if n < width:
                    at, row = picked[n]
                    eval_tile(at, row, rows, own_pos, places, tiles.at[n, 0:rows])
                if n > 0:
                    at, row = picked[n - 1]
                    add_product(at, row, rows, tiles[n - 1, 0:rows], weights, total)

        in_batches(tasks, rows, skip[rows] if skip else 0, length(tasks, rows), some)


def keep_tiles(tasks, own_pos, places, kept):
    for rows in (LONG, SHORT):

        def some(first, width, rows=rows):
            for n in range(width):
                at, row = step_at(tasks, rows, first + n)
                eval_tile(at, row, rows, own_pos, places, kept[rows].at[first + n])

        in_batches(tasks, rows, 0, jnp.minimum(length(tasks, rows), KEPT[rows]), some)


def run_kept(tasks, kept, weights, total):
    for rows in (LONG, SHORT):

        def some(first, width, rows=rows):
            for n in range(width):
                at, row = step_at(tasks, rows, first + n)
                add_product(at, row, rows, kept[rows][first + n], weights, total)

        in_batches(tasks, rows, 0, jnp.minimum(length(tasks, rows), KEPT[rows]), some)


def own_rows(o):
    return slice(o * PADDED, o * PADDED + STARS)


def padding(o):
    return slice(o * PADDED + STARS, (o + 1) * PADDED)


def stage_own_sum(own_sum, total):
    for o in range(BLOCKS):
        total[own_rows(o), :] = own_sum[o * STARS : (o + 1) * STARS, :]
        total[padding(o), :] = jnp.zeros((PADDED - STARS, LANES), F32)


def image_of(total, own_pos, vector):
    left = left_half(STARS)
    noise = jnp.where(left, own_pos[NOISE, own_rows(0), :], own_pos[NOISE, own_rows(1), :])
    return noise * vector + jnp.where(left, fold(total[own_rows(0), :]), fold(total[own_rows(1), :]))


def stage_places(device, d, places):
    for b in range(BLOCKS):
        for jc in range(CHUNKS):
            places[(BLOCKS * d + b) * CHUNKS + jc, 0:META, :] = device[meta_rows(b, jc), :]


def own_kernel(packed, noise, own_pos, own_sum, places, own_tasks, weights, total, tiles, *scratch):
    turned, lists, sem = scratch
    stage_places(packed, 0, places)
    for o in range(BLOCKS):
        for c in range(NOISE + 1):
            for ic in range(CHUNKS):
                first = o * PADDED + ic * LANES
                at = o * CHUNKS + ic
                row = noise[at : at + 1, :] if c == NOISE else places[at, c : c + 1, :]
                own_pos[c, first : first + LANES, :] = column(row)
            own_pos[c, padding(o), :] = jnp.zeros((PADDED - STARS, LANES), F32)
    build_lists(places, BLOCKS, 0, lambda o: own_pos[2, own_rows(o), :], lambda e: e >= 0, lists, turned)
    copy = pltpu.make_async_copy(lists, own_tasks, sem)
    copy.start()
    stage_weights(packed, 0, weights)
    total[...] = jnp.zeros(total.shape, F32)
    copy.wait()
    run_steps(own_tasks, own_pos, places, weights, total, tiles)
    for o in range(BLOCKS):
        own_sum[o * STARS : (o + 1) * STARS, :] = total[own_rows(o), :]


def first_kernel(
    low, mid, high, own_pos, own_sum, image_ref, places, tasks, weights, total, tiles, *scratch
):
    turned, lists, sem = scratch
    groups = (low, mid, high)
    devices = [groups[d // 3].at[d % 3] for d in range(9)]
    for d, device in enumerate(devices):
        stage_places(device, d, places)

    def others(entry):
        return (entry < OWN * CHUNKS) | (entry >= (OWN + BLOCKS) * CHUNKS)

    build_lists(places, NEAR, OWN, lambda o: own_pos[2, own_rows(o), :], others, lists, turned)
    copy = pltpu.make_async_copy(lists, tasks, sem)
    copy.start()
    for d, device in enumerate(devices):
        if d != OWN // BLOCKS:
            stage_weights(device, d, weights)
    stage_own_sum(own_sum, total)
    copy.wait()
    run_steps(tasks, own_pos, places, weights, total, tiles)
    image_ref[...] = image_of(total, own_pos, mid[1, 0:STARS, :])


def between_kernel(
    own_tasks, tasks, once, own_pos, own_places, places, own_sum, kept_long, kept_short, weights, total, tiles
):
    stage_weights(once, 0, weights)
    total[...] = jnp.zeros(total.shape, F32)
    run_steps(own_tasks, own_pos, own_places, weights, total, tiles)
    for o in range(BLOCKS):
        own_sum[o * STARS : (o + 1) * STARS, :] = total[own_rows(o), :]
    keep_tiles(tasks, own_pos, places, {LONG: kept_long, SHORT: kept_short})


def second_kernel(
    tasks,
    low,
    mid,
    high,
    own_pos,
    own_sum,
    places,
    kept_long,
    kept_short,
    packed,
    rank,
    image_ref,
    moments_ref,
    weights,
    total,
    tiles,
    sums,
):
    groups = (low, mid, high)
    for d in range(9):
        if d != OWN // BLOCKS:
            stage_weights(groups[d // 3].at[d % 3], d, weights)
    stage_own_sum(own_sum, total)
    run_kept(tasks, {LONG: kept_long, SHORT: kept_short}, weights, total)
    run_steps(tasks, own_pos, places, weights, total, tiles, skip=KEPT)
    start, once = packed[0:STARS, :], mid[1]
    twice = image_of(total, own_pos, once)
    products = (start * start, start * once, once * once, start * twice, once * twice)
    sums[...] = jnp.zeros(sums.shape, F32)
    for n, product in enumerate(products):
        sums[n : n + 1, :] = jnp.sum(product, axis=0, keepdims=True)
    top, middle, rest = (part.astype(F32) for part in split_three(fold(sums[...])))
    moments_ref[...] = jnp.where(left_half(8), top, middle)
    for n in range(3):
        pair = jnp.where(left_half(1), rest[2 * n : 2 * n + 1, :], rest[2 * n + 1 : 2 * n + 2, :])
        moments_ref[5 + n : 6 + n, :] = pair
    unsort(twice, rank, image_ref)


def unsort_kernel(x_ref, rank_ref, out_ref):
    unsort(x_ref[...], rank_ref, out_ref)


def two_sum(a, b):
    s = a + b
    back = s - a
    return s, (a - (s - back)) + (b - back)


def halves(a):
    scaled = 4097.0 * a
    top = scaled - (scaled - a)
    return top, a - top


def two_product(a, b):
    p = a * b
    a1, a2 = halves(a)
    b1, b2 = halves(b)
    return p, ((a1 * b1 - p) + a1 * b2 + a2 * b1) + a2 * b2


def pair_add(a, b):
    s, e = two_sum(a[0], b[0])
    return two_sum(s, e + (a[1] + b[1]))


def pair_mul(a, b):
    p, e = two_product(a[0], b[0])
    return two_sum(p, e + (a[0] * b[1] + a[1] * b[0]))


def final_kernel(moments_ref, start_ref, once_ref, twice_ref, solution_ref, residual_ref):
    gathered = moments_ref[...]
    rolled = pltpu.roll(gathered, WIDTH, axis=1)
    left = iota((1, LANES), 1) < WIDTH
    moments = []
    for n in range(5):
        source = gathered if n % 2 == 0 else rolled
        last = source[5 + n // 2 : 6 + n // 2, :]
        s, e = two_sum(gathered[n : n + 1, :], rolled[n : n + 1, :])
        s, e = two_sum(s, e + last)
        moments.append((jnp.where(left, s, 1.0), jnp.where(left, e, 0.0)))
    norm, curve, square, cross, cube = moments
    alpha = norm[0] / curve[0]
    step = (alpha, jnp.zeros_like(alpha))
    minus = (-alpha, jnp.zeros_like(alpha))
    step_sq = pair_mul(step, step)
    by_curve = pair_mul(minus, curve)
    norm_next = pair_add(pair_add(norm, pair_add(by_curve, by_curve)), pair_mul(step_sq, square))
    beta = norm_next[0] / norm[0]
    gamma = two_sum(jnp.ones_like(beta), beta)
    curve_next = pair_add(
        pair_mul(pair_mul(gamma, gamma), curve),
        pair_add(
            pair_mul(pair_mul(gamma, minus), pair_add(cross, square)),
            pair_mul(step_sq, cube),
        ),
    )
    alpha_next = norm_next[0] / curve_next[0]
    alpha, beta, alpha_next = (column(row)[0:WIDTH] for row in (alpha, beta, alpha_next))
    for o in range(BLOCKS):
        for ic in range(CHUNKS):
            at = (o, slice(None), lanes(ic))
            start, once, twice = start_ref[at], once_ref[at], twice_ref[at]
            residual = start - alpha * once
            direction = residual + beta * start
            image = (once - alpha * twice) + beta * once
            solution_ref[at] = alpha * start + alpha_next * direction
            residual_ref[at] = residual - alpha_next * image


def shape(*dims, dtype=F32):
    return jax.ShapeDtypeStruct(dims, dtype)


def call(kernel, out_shape, scratch=(), in_specs=None, count=None, out_specs=None, limit=LIMIT, flops=0, nbytes=1 << 20):
    return pl.pallas_call(
        kernel,
        out_shape=out_shape,
        in_specs=in_specs if in_specs is not None else [VMEM] * count,
        out_specs=out_specs or jax.tree.map(lambda _: VMEM, out_shape),
        scratch_shapes=list(scratch),
        compiler_params=pltpu.CompilerParams(vmem_limit_bytes=limit),
        cost_estimate=pl.CostEstimate(flops=flops, bytes_accessed=nbytes, transcendentals=0),
    )


BLOCK = shape(BLOCKS, WIDTH, STARS)
OWN_POS = shape(NOISE + 1, BLOCKS * PADDED, LANES)
OWN_SUM = shape(BLOCKS * STARS, LANES)
TASKS = shape(8, LANES, dtype=jnp.int32)


def pairs_scratch(blocks):
    return [
        pltpu.VMEM((blocks * CHUNKS, LANES, LANES), BF16),
        pltpu.VMEM((BLOCKS * PADDED, LANES), F32),
        pltpu.VMEM((max(AT_ONCE.values()), LONG, 2 * LANES), BF16),
    ]


LIST_SCRATCH = [
    pltpu.VMEM((2, LANES, LANES), F32),
    pltpu.VMEM((8, LANES), jnp.int32),
    pltpu.SemaphoreType.DMA,
]


def apply_own(packed, noise):
    return call(
        own_kernel,
        (OWN_POS, OWN_SUM, shape(BLOCKS * CHUNKS, 8, LANES), TASKS),
        scratch=pairs_scratch(BLOCKS) + LIST_SCRATCH,
        count=2,
        out_specs=(VMEM, VMEM, VMEM, SMEM),
        flops=1 << 30,
    )(packed, noise)


def apply_first(low, mid, high, own_pos, own_sum):
    return call(
        first_kernel,
        (shape(STARS, LANES), shape(NEAR * CHUNKS, 8, LANES), TASKS),
        scratch=pairs_scratch(NEAR) + LIST_SCRATCH,
        count=5,
        out_specs=(VMEM, VMEM, SMEM),
    )(low, mid, high, own_pos, own_sum)


def apply_between(own_tasks, tasks, once, own_pos, own_places, places):
    return call(
        between_kernel,
        (
            OWN_SUM,
            shape(KEPT[LONG], LONG, 2 * LANES, dtype=BF16),
            shape(KEPT[SHORT], SHORT, 2 * LANES, dtype=BF16),
        ),
        scratch=pairs_scratch(BLOCKS),
        in_specs=[SMEM, SMEM] + [VMEM] * 4,
        flops=1 << 30,
    )(own_tasks, tasks, once, own_pos, own_places, places)


def apply_second(tasks, low, mid, high, own_pos, own_sum, places, kept_long, kept_short, packed, rank):
    return call(
        second_kernel,
        (BLOCK, shape(8, LANES)),
        scratch=pairs_scratch(NEAR) + [pltpu.VMEM((8, LANES), F32)],
        in_specs=[SMEM] + [VMEM] * 10,
    )(tasks, low, mid, high, own_pos, own_sum, places, kept_long, kept_short, packed, rank)


def shift(x, axis, by):
    count = lax.axis_size(axis)
    return lax.ppermute(x, axis, [(i, i + by) for i in range(count) if 0 <= i + by < count])


SKY = ("far", "near", "x", "core")


def sky_shift(x, by):
    count = lax.axis_size(SKY)
    return lax.ppermute(x, SKY, [(i, i + by) for i in range(count) if 0 <= i + by < count])


def with_halo(x):
    before, after = shift(x, "tm", 1), shift(x, "tm", -1)
    mid = lax.optimization_barrier(jnp.zeros((3,) + x.shape, F32).at[1].set(x))
    mid = mid.at[0].set(before).at[2].set(after)
    return sky_shift(mid, 1), mid, sky_shift(mid, -1)


def local(star_pos, noise_var, targets, pair_list):
    ident = (lax.axis_index(SKY) * lax.axis_size("tm") + lax.axis_index("tm")) * BLOCKS
    hbm = pl.BlockSpec(memory_space=pltpu.HBM)
    stars = (BLOCKS, STARS)
    packed, rank, noise = call(
        sort_kernel,
        (shape(ROWS, LANES), shape(*stars), shape(BLOCKS * CHUNKS, LANES)),
        scratch=[
            pltpu.VMEM((BLOCKS * WIDTH, STARS), F32),
            pltpu.VMEM((16, STARS), F32),
            pltpu.VMEM((3,) + stars, F32),
            pltpu.VMEM(stars, F32),
            pltpu.VMEM((BLOCKS, WIDTH, STARS), F32),
            pltpu.VMEM(pair_list.shape, jnp.int32),
            pltpu.SemaphoreType.DMA((4,)),
        ],
        in_specs=[SMEM] + [hbm] * 4,
        limit=FULL - 512 * 1024,
    )(ident.reshape(1), jnp.swapaxes(star_pos, 0, 1), noise_var, targets, pair_list)
    low, mid, high = with_halo(packed)
    own_pos, own_sum, own_places, own_tasks = apply_own(packed, noise)
    once, places, tasks = apply_first(low, mid, high, own_pos, own_sum)
    low, mid, high = with_halo(once)
    own_sum, *kept = apply_between(own_tasks, tasks, once, own_pos, own_places, places)
    once_back = call(unsort_kernel, BLOCK, count=2, flops=1 << 28)(once, rank)
    twice_back, moments = apply_second(
        tasks, low, mid, high, own_pos, own_sum, places, *kept, packed, rank
    )
    for axis in ("core", "x", "tm", "near", "far"):
        moments = lax.psum(moments, axis)
    return call(final_kernel, (BLOCK, BLOCK), count=4)(moments, targets, once_back, twice_back)


def solution(mesh):
    sky, tm = mesh.devices.shape
    near = 4 if sky % 32 == 0 else 1
    finer = Mesh(mesh.devices.reshape(sky // (8 * near), near, 4, 2, tm), SKY + ("tm",))
    both = SKY + ("tm",)
    in_specs = (P(both, None, None), P(both, None), P(both, None, None), P(both, None))
    out_specs = (P(both, None, None), P(both, None, None))
    return jax.shard_map(local, mesh=finer, in_specs=in_specs, out_specs=out_specs, check_vma=False)
```
